256 devices in a mesh: grid: 64 (over z, y, core), layer: 4 (over x).
Axes of the slice: x: 4, y: 4, z: 8, core: 2. Of those that a mesh axis runs over, the one named last changes fastest.
Arguments:
- x_blocks: bfloat16 [4096, 128, 128], P('grid'), may hold values from -0.3984375 to 0.3984375
- send_first: int32 [64, 4, 64, 1], P('grid', 'layer'), may hold values from 0 to 63
- send_left: int32 [64, 4, 64, 1], P('grid', 'layer'), may hold values from 0 to 63
- send_right: int32 [64, 64, 1], P('grid'), may hold values from 0 to 63
- terms_first: int32 [4096, 4, 12, 2], P('grid', 'layer'), may hold values from 0 to 63
- terms_second: int32 [4096, 4, 12, 2], P('grid', 'layer'), may hold values from 0 to 63
- live_first: int32 [4096, 4], P('grid', 'layer'), may hold values from 1 to 12, as said below
- live_second: int32 [4096, 4], P('grid', 'layer'), may hold values from 1 to 12, as said below
Outputs:
- square: bfloat16 [4096, 128, 128], P('grid', 'layer')
- sign_step: bfloat16 [4096, 128, 128], P('grid', 'layer')
The draws below stay inside these ranges and needn't reach their ends.
Inputs may be any that keep to these rules, and one draw needn't show every extreme that they name: `live_first`: number of live term slots of an output block on one layer; later slots are unused. `live_second`: number of live term slots of an output block on one layer; later slots are unused.
All inputs are finite; a program needn't handle non-finite values.
Results may differ from the reference program's by a relative error of at most 0.015.
Values may be sent and summed in bfloat16 or wider, within the bound.
A program may use at most 128 MiB of HBM per device.

```python
import jax
import jax.numpy as jnp
from jax import lax

B = 128
BLK_DEV = 64
TPO = 12
CAP = 1
NNZ = 4096
SLOTS = 64
N_GRID = 64
N_LAYER = 4


def skewed_counts(key):
    cap_key, heavy_key, spot_key, count_key = jax.random.split(key, 4)
    bound_cap = jax.random.randint(cap_key, (N_GRID, N_LAYER), max(1, TPO // 4), TPO + 1)
    heavy_device = jax.random.randint(heavy_key, (), 0, N_GRID * N_LAYER)
    device_ids = jnp.arange(N_GRID * N_LAYER, dtype=jnp.int32).reshape(N_GRID, N_LAYER)
    bound_cap = jnp.where(device_ids == heavy_device, TPO, bound_cap)
    spread = jnp.repeat(bound_cap, BLK_DEV, axis=0)
    counts = jax.random.randint(count_key, (NNZ, N_LAYER), 1, spread + 1)
    heavy_slot = jax.random.randint(spot_key, (), 0, BLK_DEV)
    row_ids = jnp.arange(NNZ, dtype=jnp.int32)[:, None]
    layer_ids = jnp.arange(N_LAYER, dtype=jnp.int32)[None, :]
    chosen = (row_ids == heavy_device // N_LAYER * BLK_DEV + heavy_slot) & (layer_ids == heavy_device % N_LAYER)
    return jnp.where(chosen, TPO, counts).astype(jnp.int32)


def draw_live_first(key, part):
    key = jax.random.fold_in(key, 11)
    return skewed_counts(key)


def draw_live_second(key, part):
    key = jax.random.fold_in(key, 23)
    return skewed_counts(key)


def touch_ends(array, stream_key, smallest, largest):
    longest = array.shape.index(max(array.shape))
    spots = []
    for shift in (0, 1):
        where = [jax.random.randint(jax.random.fold_in(stream_key, axis), (), 0, length) for axis, length in enumerate(array.shape)]
        where[longest] = (where[longest] + shift) % array.shape[longest]
        spots.append(tuple(where))
    return array.at[spots[0]].set(smallest).at[spots[1]].set(largest)


def levels(key, shape, shards, least, top_value):
    gain = 1.0
    for position, shards_of in shards:
        steps = jax.random.uniform(jax.random.fold_in(jax.random.fold_in(key, 6), position), (shards_of,), jnp.float32, least / len(shards), top_value / len(shards))
        gain = gain * jnp.repeat(jnp.exp(steps), shape[position] // shards_of).reshape((-1,) + (1,) * (len(shape) - 1 - position))
    return gain


def noise(own_key, shape, width, bound, cuts=(), kind=jnp.bfloat16):
    entries = width * jax.random.normal(own_key, shape, jnp.float32)
    if cuts:
        entries = entries * levels(own_key, shape, cuts, -0.22, 0.18)
    return jnp.clip(entries, -bound, bound).astype(kind)


def setup_inputs(seed: int = 0) -> dict:
    streams_of = jax.random.split(jax.random.key(seed), 9)
    return {
        "x_blocks": noise(streams_of[0], (NNZ, B, B), 0.05, 0.3984375, ((0, 64),)),
        "send_first": touch_ends(jax.random.randint(streams_of[1], (N_GRID, N_LAYER, N_GRID, CAP), 0, BLK_DEV), jax.random.fold_in(streams_of[1], 1), 0, BLK_DEV - 1).astype(jnp.int32),
        "send_left": touch_ends(jax.random.randint(streams_of[2], (N_GRID, N_LAYER, N_GRID, CAP), 0, BLK_DEV), jax.random.fold_in(streams_of[2], 1), 0, BLK_DEV - 1).astype(jnp.int32),
        "send_right": touch_ends(jax.random.randint(streams_of[3], (N_GRID, N_GRID, CAP), 0, BLK_DEV), jax.random.fold_in(streams_of[3], 1), 0, BLK_DEV - 1).astype(jnp.int32),
        "terms_first": touch_ends(jax.random.randint(streams_of[4], (NNZ, N_LAYER, TPO, 2), 0, SLOTS), jax.random.fold_in(streams_of[4], 1), 0, SLOTS - 1).astype(jnp.int32),
        "terms_second": touch_ends(jax.random.randint(streams_of[5], (NNZ, N_LAYER, TPO, 2), 0, SLOTS), jax.random.fold_in(streams_of[5], 1), 0, SLOTS - 1).astype(jnp.int32),
        "live_first": draw_live_first(jax.random.fold_in(streams_of[8], 71), 0),
        "live_second": draw_live_second(jax.random.fold_in(streams_of[8], 71), 0),
    }


def layered_table(sends, slot_base):
    shifted = jnp.transpose(sends, (2, 1, 0, 3)) + slot_base[None, None, :, None]
    return jnp.reshape(shifted, (N_GRID, N_LAYER, N_GRID * CAP)).astype(jnp.int32)


def layer_term(left_source, right_source, left_table, right_table, terms, live):
    owner_device = jnp.arange(NNZ, dtype=jnp.int32) // BLK_DEV
    left_ids = left_table[owner_device[:, None], terms[:, :, 0]]
    right_ids = right_table[owner_device[:, None], terms[:, :, 1]]
    left_groups = left_ids.reshape(N_GRID, BLK_DEV, TPO)
    right_groups = right_ids.reshape(N_GRID, BLK_DEV, TPO)
    live_groups = live.reshape(N_GRID, BLK_DEV)

    def one_group(packed):
        left_pick, right_pick, alive_count = packed
        keep_mask = (jnp.arange(TPO, dtype=jnp.int32)[None, :] < alive_count[:, None]).astype(jnp.float32)
        left_stack = left_source[left_pick].astype(jnp.float32) * keep_mask[:, :, None, None]
        right_stack = right_source[right_pick].astype(jnp.float32)
        return jnp.einsum("gtij,gtjk->gik", left_stack, right_stack)

    result = lax.map(one_group, (left_groups, right_groups, live_groups))
    return result.reshape(NNZ, B, B)


def reference(x_blocks, send_first, send_left, send_right, terms_first, terms_second, live_first, live_second):
    slot_base = jnp.arange(N_GRID, dtype=jnp.int32) * BLK_DEV
    first_table = layered_table(send_first, slot_base)
    left_table = layered_table(send_left, slot_base)
    right_table = jnp.reshape(jnp.transpose(send_right, (1, 0, 2)) + slot_base[None, :, None], (N_GRID, N_GRID * CAP)).astype(jnp.int32)
    product_sum = jnp.zeros((NNZ, B, B), jnp.float32)
    for layer_index in range(N_LAYER):
        first_term = layer_term(x_blocks, x_blocks, first_table[:, layer_index], first_table[:, layer_index], terms_first[:, layer_index], live_first[:, layer_index])
        rounded = lax.optimization_barrier(first_term.astype(jnp.bfloat16))
        product_sum = product_sum + rounded.astype(jnp.float32)
    square = product_sum.astype(jnp.bfloat16)
    update_sum = jnp.zeros((NNZ, B, B), jnp.float32)
    for layer_index in range(N_LAYER):
        update_sum = update_sum + layer_term(x_blocks, square, left_table[:, layer_index], right_table, terms_second[:, layer_index], live_second[:, layer_index])
    sign_step = (1.5 * x_blocks.astype(jnp.float32) - 0.5 * update_sum).astype(jnp.bfloat16)
    return square, sign_step
```

```python
import functools

import jax
import jax.numpy as jnp
from jax import lax
from jax.experimental import pallas as pl
from jax.experimental.pallas import tpu as pltpu
from jax.sharding import PartitionSpec as P

MESH = pl.DeviceIdType.MESH
BF = jnp.bfloat16
F32 = jnp.float32
HALF = 64
CHUNKS = 4
ROWS = 16


def kernel(
    grid_n,
    y_n,
    blocks,
    terms,
    idx_ref,
    tab_ref,
    x_ref,
    sq_ref,
    out_ref,
    stage,
    lstage,
    rstage,
    first,
    left,
    right,
    part,
    part2,
    rs1,
    rs2,
    comb1,
    comb2,
    tabs,
    stab,
    send_sem,
    recv_sem,
    tab_send,
    tab_recv,
    loc_sem,
    rs_send,
    rs_recv,
):
    me = lax.axis_index("grid")
    lay = lax.axis_index("layer")
    width = x_ref.shape[1]
    quarter = width // 4
    z_n = grid_n // (2 * y_n)
    z, y, core = me // (2 * y_n), (me // 2) % y_n, me % 2
    per = blocks // CHUNKS

    def peer(i):
        dz, m = ((i % z_n) * 5) % z_n, i // z_n
        dy, dc = m // 2, m % 2
        return ((z + dz) % z_n) * (2 * y_n) + ((y + dy) % y_n) * 2 + (core + dc) % 2

    barrier = pltpu.get_barrier_semaphore()

    def greet(i, carry):
        pl.semaphore_signal(barrier, inc=1, device_id=(peer(i), lay), device_id_type=MESH)
        return carry

    lax.fori_loop(1, grid_n, greet, 0)
    for step in range(1, 4):
        pl.semaphore_signal(
            barrier, inc=1, device_id=(me, (lay + step) % 4), device_id_type=MESH
        )

    def fill_first(i, carry):
        stage[i] = x_ref[idx_ref[terms, peer(i)]]
        return carry

    lax.fori_loop(0, grid_n, fill_first, 0)
    first[me] = stage[0]
    first[grid_n] = jnp.zeros((width, width), BF)
    left[grid_n] = jnp.zeros((width, width), BF)
    tabs[lay] = tab_ref[...]
    pl.semaphore_wait(barrier, grid_n - 1 + 3)

    def tab_copy(step):
        return pltpu.make_async_remote_copy(
            src_ref=tab_ref,
            dst_ref=tabs.at[lay],
            send_sem=tab_send.at[step - 1],
            recv_sem=tab_recv.at[step - 1],
            device_id=(me, (lay + step) % 4),
            device_id_type=MESH,
        )

    for step in range(1, 4):
        tab_copy(step).start()

    def spread(src, dst, which):
        def one(i, carry):
            pltpu.make_async_remote_copy(
                src_ref=src.at[i],
                dst_ref=dst.at[me],
                send_sem=send_sem.at[which],
                recv_sem=recv_sem.at[which],
                device_id=(peer(i), lay),
                device_id_type=MESH,
            ).start()
            return carry

        lax.fori_loop(1, grid_n, one, 0)

    def wait_all(src, sem):
        whole = src.at[pl.ds(1, grid_n - 1)]
        pltpu.make_async_copy(whole, whole, sem).wait()

    spread(stage, first, 0)

    for step in range(1, 4):
        tab_copy(step).wait_recv()
    to_smem = pltpu.make_async_copy(tabs, stab, loc_sem)
    to_smem.start()
    to_smem.wait()

    lane = lax.broadcasted_iota(jnp.int32, (width, width), 1) // quarter
    sub = lax.broadcasted_iota(jnp.int32, (width, width), 0)
    lane_all = lax.broadcasted_iota(jnp.int32, (width, width), 1)
    picks = [
        ((sub == lay * quarter + lane_all - j * quarter) & (lane == j)).astype(BF)
        for j in range(4)
    ]
    pick = jnp.concatenate(picks, axis=0)

    def fill_left(i, carry):
        d = peer(i)
        rows = jnp.concatenate([x_ref[stab[j, terms, d]] for j in range(4)], axis=1)
        lstage[i] = jnp.dot(rows, pick, preferred_element_type=F32).astype(BF)
        return carry

    lax.fori_loop(0, grid_n, fill_left, 0)
    left[me] = lstage[0]
    wait_all(stage, send_sem.at[0])
    spread(lstage, left, 1)
    wait_all(stage, recv_sem.at[0])

    right_lay, left_lay, far_lay = (lay + 1) % 4, (lay + 3) % 4, (lay + 2) % 4

    def rows_of(q, h):
        return pl.ds(pl.multiple_of(q * quarter + h * ROWS, ROWS), ROWS)

    def reduce_rows(phase, product, src, got, comb, finish):
        def copy(kind, c):
            span = pl.ds(c * per, per)
            if kind == 0:
                ref, to = src.at[span, rows_of(far_lay, 0)], right_lay
            elif kind == 1:
                ref, to = src.at[span, rows_of(far_lay, 1)], left_lay
            elif kind == 2:
                ref, to = src.at[span, rows_of(right_lay, 1)], right_lay
            elif kind == 3:
                ref, to = src.at[span, rows_of(left_lay, 0)], left_lay
            elif kind == 4:
                ref, to = comb.at[0, span], right_lay
            else:
                ref, to = comb.at[1, span], left_lay
            return pltpu.make_async_remote_copy(
                src_ref=ref,
                dst_ref=got.at[kind, span],
                send_sem=rs_send.at[phase, kind, c],
                recv_sem=rs_recv.at[phase, kind, c],
                device_id=(me, to),
                device_id_type=MESH,
            )

        def relay(c):
            span = pl.ds(c * per, per)
            for kind, q in ((0, right_lay), (1, left_lay)):
                copy(kind, c).wait_recv()
                own = src[span, rows_of(q, kind)].astype(F32)
                comb[kind, span] = (own + got[kind, span].astype(F32)).astype(BF)
                copy(4 + kind, c).start()

        def chunk(c, carry):
            def one(o, inner):
                product(o)
                return inner

            lax.fori_loop(c * per, (c + 1) * per, one, 0)
            for kind in range(4):
                copy(kind, c).start()

            @pl.when(c >= 1)
            def _():
                relay(c - 1)

            return carry

        lax.fori_loop(0, CHUNKS, chunk, 0)
        relay(CHUNKS - 1)

        def close(c, carry):
            span = pl.ds(c * per, per)
            for h, direct, joined in ((0, 3, 4), (1, 2, 5)):
                copy(direct, c).wait_recv()
                copy(joined, c).wait_recv()
                total = (
                    src[span, rows_of(lay, h)].astype(F32)
                    + got[direct, span].astype(F32)
                    + got[joined, span].astype(F32)
                )
                finish(span, h, total)
            return carry

        lax.fori_loop(0, CHUNKS, close, 0)

        def drain(c, carry):
            for kind in range(6):
                copy(kind, c).wait_send()
            return carry

        return drain

    def product_first(o):
        acc = jnp.zeros((width, width), F32)
        for t in range(0, terms, 2):
            a = jnp.concatenate([first[idx_ref[u, o]] for u in (t, t + 1)], axis=1)
            b = jnp.concatenate([first[idx_ref[u, HALF + o]] for u in (t, t + 1)], axis=0)
            acc = acc + jnp.dot(a, b, preferred_element_type=F32)
        part[o] = acc.astype(BF)

    def finish_first(span, h, total):
        sq_ref[span, pl.ds(h * ROWS, ROWS)] = total.astype(BF)

    drain_first = reduce_rows(0, product_first, part, rs1, comb1, finish_first)

    def fill_right(i, carry):
        rstage[i] = sq_ref[idx_ref[terms, HALF + peer(i)]]
        return carry

    lax.fori_loop(0, grid_n, fill_right, 0)
    right[me] = rstage[0]
    spread(rstage, right, 2)
    wait_all(lstage, recv_sem.at[1])
    wait_all(rstage, recv_sem.at[2])

    def product_second(o):
        acc = jnp.zeros((width, width), F32)
        for t in range(0, terms, 2):
            a_parts, b_parts = [], []
            for u in (t, t + 1):
                lefts = [left[stab[j, u, o]] for j in range(4)]
                low = jnp.where(lane == 0, lefts[0], lefts[1])
                high = jnp.where(lane == 2, lefts[2], lefts[3])
                a_parts.append(jnp.where(lane < 2, low, high))
                b_parts += [right[stab[j, u, HALF + o]] for j in range(4)]
            a = jnp.concatenate(a_parts, axis=1)
            b = jnp.concatenate(b_parts, axis=0)
            acc = acc + jnp.dot(a, b, preferred_element_type=F32)
        part2[o] = acc.astype(BF)

    def finish_second(span, h, total):
        own = x_ref[span, rows_of(lay, h)].astype(F32)
        out_ref[span, pl.ds(h * ROWS, ROWS)] = (1.5 * own - 0.5 * total).astype(BF)

    drain_second = reduce_rows(1, product_second, part2, rs2, comb2, finish_second)

    lax.fori_loop(0, CHUNKS, drain_first, 0)
    lax.fori_loop(0, CHUNKS, drain_second, 0)
    for step in range(1, 4):
        tab_copy(step).wait_send()
    wait_all(lstage, send_sem.at[1])
    wait_all(rstage, send_sem.at[2])


def term_table(terms, live, extra, slots):
    blocks, count = terms.shape[0], terms.shape[2]
    pairs = terms.reshape(blocks, count, 2)
    keep = lax.broadcasted_iota(jnp.int32, (blocks, count), 1) < live.reshape(blocks, 1)
    lefts = jnp.where(keep, pairs[:, :, 0], slots)
    rows = jnp.stack([lefts, pairs[:, :, 1]], axis=0)
    rows = jnp.pad(rows.transpose(2, 0, 1), ((0, 0), (0, 0), (0, HALF - blocks)))
    table = jnp.concatenate([rows.reshape(count, 2 * HALF), extra.reshape(1, 2 * HALF)], axis=0)
    return jnp.pad(table, ((0, 16 - count - 1), (0, 0)))


def local(
    y_n,
    x_blocks,
    send_first,
    send_left,
    send_right,
    terms_first,
    terms_second,
    live_first,
    live_second,
):
    grid_n = lax.axis_size("grid")
    blocks, width = x_blocks.shape[0], x_blocks.shape[1]
    count = terms_first.shape[2]
    quarter = width // 4

    def padded(slots):
        flat = slots.reshape(-1)
        return jnp.pad(flat, (0, HALF - flat.shape[0]))

    extra_first = jnp.concatenate([padded(send_first), padded(send_right)])
    extra_second = jnp.concatenate([padded(send_left), padded(send_left)])
    idx = term_table(terms_first, live_first, extra_first, grid_n)
    tab = term_table(terms_second, live_second, extra_second, grid_n)
    share = jax.ShapeDtypeStruct((blocks, quarter, width), BF)
    vmem = pl.BlockSpec(memory_space=pltpu.VMEM)
    dma = pltpu.SemaphoreType.DMA
    return pl.pallas_call(
        functools.partial(kernel, grid_n, y_n, blocks, count),
        out_shape=(share, share),
        in_specs=[pl.BlockSpec(memory_space=pltpu.SMEM), vmem, vmem],
        out_specs=(vmem, vmem),
        scratch_shapes=[
            pltpu.VMEM((grid_n, width, width), BF),
            pltpu.VMEM((grid_n, width, width), BF),
            pltpu.VMEM((grid_n, quarter, width), BF),
            pltpu.VMEM((grid_n + 1, width, width), BF),
            pltpu.VMEM((grid_n + 1, width, width), BF),
            pltpu.VMEM((grid_n, quarter, width), BF),
            pltpu.VMEM((blocks, width, width), BF),
            pltpu.VMEM((blocks, width, width), BF),
            pltpu.VMEM((6, blocks, ROWS, width), BF),
            pltpu.VMEM((6, blocks, ROWS, width), BF),
            pltpu.VMEM((2, blocks, ROWS, width), BF),
            pltpu.VMEM((2, blocks, ROWS, width), BF),
            pltpu.VMEM((4, 16, 128), jnp.int32),
            pltpu.SMEM((4, 16, 128), jnp.int32),
            dma((3,)),
            dma((3,)),
            dma((3,)),
            dma((3,)),
            dma,
            dma((2, 6, CHUNKS)),
            dma((2, 6, CHUNKS)),
        ],
        compiler_params=pltpu.CompilerParams(
            collective_id=0, has_side_effects=True, vmem_limit_bytes=48 * 1024 * 1024
        ),
    )(idx, tab, x_blocks)


def solution(mesh, y_n=4):
    return jax.shard_map(
        functools.partial(local, y_n),
        mesh=mesh,
        in_specs=(
            P("grid", None, None),
            P("grid", "layer", None, None),
            P("grid", "layer", None, None),
            P("grid", None, None),
            P("grid", "layer", None, None),
            P("grid", "layer", None, None),
            P("grid", "layer"),
            P("grid", "layer"),
        ),
        out_specs=(P("grid", "layer", None), P("grid", "layer", None)),
        check_vma=False,
    )
```

```python
import functools

import jax
import jax.numpy as jnp
from jax import lax
from jax.experimental import pallas as pl
from jax.experimental.pallas import tpu as pltpu
from jax.sharding import PartitionSpec as P

MESH = pl.DeviceIdType.MESH
BF = jnp.bfloat16
F32 = jnp.float32
HALF = 64
CHUNKS = 8
LAG = 2
FAR_FIRST = (4, 3, 5, 2, 6, 1, 7)
ROWS = 16
SUBS = 2


def slot_order(k, n):
    k = k % n
    return 0 if k == 0 else (2 * k - 1 if 2 * k <= n else 2 * (n - k))


def kernel(
    grid_n,
    y_n,
    blocks,
    terms,
    x_hbm,
    sf_ref,
    sl_ref,
    ssr,
    tf_ref,
    ts_ref,
    lf_ref,
    ls_ref,
    sq_ref,
    out_ref,
    x_ref,
    *refs,
):
    near_n = 2 * (grid_n // (2 * y_n) // 4) + 1
    gathered = refs[:near_n]
    run(
        grid_n, y_n, blocks, terms, x_hbm, sf_ref, sl_ref, ssr, tf_ref, ts_ref, lf_ref, ls_ref,
        sq_ref, out_ref, x_ref, gathered, *refs[near_n:]
    )


def run(
    grid_n,
    y_n,
    blocks,
    terms,
    x_hbm,
    sf_ref,
    sl_ref,
    ssr,
    tf_ref,
    ts_ref,
    lf_ref,
    ls_ref,
    sq_ref,
    out_ref,
    x_ref,
    gathered,
    stage,
    lstage,
    far_out,
    far_in,
    lfar_out,
    lfar_in,
    mid,
    rstage,
    first,
    left,
    right,
    part,
    part2,
    rs1,
    rs2,
    comb1,
    comb2,
    ftab,
    sftab,
    tabs,
    stab,
    rows,
    srows,
    send_sem,
    recv_sem,
    ring_send,
    ring_recv,
    far_send,
    far_recv,
    cross_send,
    cross_recv,
    tab_send,
    tab_recv,
    row_send,
    row_recv,
    loc_sem,
    rs_send,
    rs_recv,
):
    me = lax.axis_index("grid")
    lay = lax.axis_index("layer")
    load_x = pltpu.make_async_copy(x_hbm, x_ref, loc_sem.at[0])
    load_x.start()
    width = x_ref.shape[1]
    quarter = width // 4
    z_n = grid_n // (2 * y_n)
    yc_n = 2 * y_n
    z, y, core = me // yc_n, (me // 2) % y_n, me % 2
    yc = y * 2 + core
    per = blocks // CHUNKS
    sub = blocks // SUBS
    plane_n = yc_n * 4
    half_z = z_n // 2
    reach = half_z // 2
    half_plane = plane_n // 2
    zs = [lax.rem(z + dz, z_n) * yc_n for dz in range(z_n)]
    lays = [lax.rem(lay + dx, 4) for dx in range(4)]

    def mate_yc(m):
        return lax.rem(y + lax.div(m, 2), y_n) * 2 + lax.rem(core + m, 2)

    def at_z(dz):
        return (zs[dz % z_n] + yc, lay)

    def each_peer(act):
        def one(m, carry):
            other = mate_yc(m)
            for dz in FAR_FIRST:
                if 0 < dz < z_n:
                    act(m * z_n + dz, zs[dz] + other)

            @pl.when(m > 0)
            def _():
                act(m * z_n, zs[0] + other)

            return carry

        lax.fori_loop(0, yc_n, one, 0)

    def each_mate(low, high, act):
        def one(m, carry):
            d = zs[0] + mate_yc(m)
            for dx in range(1, 4):
                act(m * 4 + dx, d, lays[dx])

            @pl.when(m > 0)
            def _():
                act(m * 4, d, lay)

            return carry

        lax.fori_loop(low, high, one, 0)

    my_rows = pl.ds(pl.multiple_of(lay * quarter, quarter), quarter)

    barrier = pltpu.get_barrier_semaphore()

    def greet(d, to):
        pl.semaphore_signal(barrier, inc=1, device_id=(d, to), device_id_type=MESH)

    each_peer(lambda i, d: greet(d, lay))

    def greet_layers(m, carry):
        d = zs[0] + mate_yc(m)
        for dx in range(1, 4):
            greet(d, lays[dx])
        return carry

    lax.fori_loop(0, yc_n, greet_layers, 0)

    def moved(slots):
        away = lax.rem(lax.div(slots, yc_n) - z + z_n, z_n)
        order = jnp.where(2 * away <= z_n, 2 * away - 1, 2 * (z_n - away))
        order = jnp.where(away == 0, 0, order)
        return lax.rem(slots, yc_n), order

    def pad_row(values):
        return jnp.pad(values, ((0, 0), (0, HALF - values.shape[1])))

    term = lax.broadcasted_iota(jnp.int32, (terms, 1, blocks), 0)
    span_o = pl.ds(0, blocks)
    for table, live, to in ((tf_ref, lf_ref, ftab), (ts_ref, ls_ref, tabs.at[lay])):
        keep = term < live[...].reshape(1, 1, blocks)
        to[...] = jnp.zeros(to.shape, jnp.int32)
        lefts, rights = table[:, pl.ds(0, 1)], table[:, pl.ds(1, 1)]
        at_yc, order = moved(lefts)
        if to is ftab:
            lefts = at_yc * z_n + order
            at_yc, order = moved(rights)
            rights = at_yc * z_n + order
        else:
            lefts = order * yc_n + at_yc
        to[:, pl.ds(0, 1), span_o] = jnp.where(keep, lefts, grid_n)
        to[:, pl.ds(1, 1), span_o] = rights
    rows[0, lay] = jnp.concatenate([pad_row(sf_ref[...]), pad_row(sl_ref[...])], axis=1)
    first[grid_n] = jnp.zeros((width, width), BF)
    left[grid_n] = jnp.zeros((width, width), BF)
    load_x.wait()
    gathered[0][...] = x_ref[:, my_rows, :]
    pl.semaphore_wait(barrier, grid_n - 1 + 3 * yc_n)

    def hop(up, k, s):
        if k == 1:
            src = 0
        else:
            src = slot_order(-(k - 1) if up else k - 1, z_n)
        dst = slot_order(-k if up else k, z_n)
        span = pl.ds(s * sub, sub)
        which = 0 if up else 1
        return pltpu.make_async_remote_copy(
            src_ref=gathered[src].at[span],
            dst_ref=gathered[dst].at[span],
            send_sem=ring_send.at[which, k - 1, s],
            recv_sem=ring_recv.at[which, k - 1, s],
            device_id=at_z(1 if up else -1),
            device_id_type=MESH,
        )

    def hops():
        return [(up, s) for s in range(SUBS) for up in (True, False)]

    def tab_copy(step):
        return pltpu.make_async_remote_copy(
            src_ref=tabs.at[lay],
            dst_ref=tabs.at[lay],
            send_sem=tab_send.at[step - 1],
            recv_sem=tab_recv.at[step - 1],
            device_id=(me, lays[step]),
            device_id_type=MESH,
        )

    def row_copy(step):
        return pltpu.make_async_remote_copy(
            src_ref=rows.at[0, lay],
            dst_ref=rows.at[0, lay],
            send_sem=row_send.at[step - 1],
            recv_sem=row_recv.at[step - 1],
            device_id=(me, lays[step]),
            device_id_type=MESH,
        )

    def rows_copy(step):
        return pltpu.make_async_remote_copy(
            src_ref=rows.at[0],
            dst_ref=rows.at[slot_order(-step, z_n)],
            send_sem=row_send.at[2 + step % z_n],
            recv_sem=row_recv.at[2 + step % z_n],
            device_id=at_z(step),
            device_id_type=MESH,
        )

    for step in range(1, 4):
        row_copy(step).start()
    for up, s in hops():
        hop(up, 1, s).start()
    for step in range(1, 4):
        tab_copy(step).start()
    for step in range(1, 4):
        row_copy(step).wait_recv()
    near = [step for k in range(1, reach + 1) for step in (k, -k)]
    for step in near:
        rows_copy(step).start()
    for step in near:
        rows_copy(step).wait_recv()
    for step in range(1, 4):
        tab_copy(step).wait_recv()
    moves = [
        pltpu.make_async_copy(rows, srows, loc_sem.at[0]),
        pltpu.make_async_copy(tabs, stab, loc_sem.at[1]),
        pltpu.make_async_copy(ftab, sftab, loc_sem.at[2]),
    ]
    for move in moves:
        move.start()
    for move in moves:
        move.wait()

    def group(k):
        if k == 0:
            return 0, 1
        return 2 * k - 1, 2

    def plane_copy(src, dst, which, low, count, d, to):
        return pltpu.make_async_remote_copy(
            src_ref=src,
            dst_ref=dst.at[pl.ds(yc * z_n + low, count), my_rows],
            send_sem=send_sem.at[which],
            recv_sem=recv_sem.at[which],
            device_id=(d, to),
            device_id_type=MESH,
        )

    def plane_send(src, dst, which, k):
        low, count = group(k)

        def one(i, d, to):
            plane_copy(src.at[i, pl.ds(low, count)], dst, which, low, count, d, to).start()

        each_mate(0, yc_n, one)
        dst[pl.ds(yc * z_n + low, count), my_rows] = src[0, pl.ds(low, count)]

    def left_direct(k):
        low, count = group(k)
        for r in range(low, low + count):
            slots = pl.ds(r * yc_n + yc, 1)

            def one(i, d, to):
                pltpu.make_async_remote_copy(
                    src_ref=lstage.at[i, pl.ds(r, 1)],
                    dst_ref=left.at[slots, my_rows],
                    send_sem=send_sem.at[1],
                    recv_sem=recv_sem.at[1],
                    device_id=(d, to),
                    device_id_type=MESH,
                ).start()

            each_mate(0, yc_n, one)
            left[slots, my_rows] = lstage[0, pl.ds(r, 1)]

    def left_across(piece, src_of):
        slot = piece * yc_n + yc

        def one(m, carry):
            pltpu.make_async_remote_copy(
                src_ref=src_of(m),
                dst_ref=mid.at[:, slot],
                send_sem=send_sem.at[3],
                recv_sem=recv_sem.at[3],
                device_id=(zs[0] + mate_yc(m), lay),
                device_id_type=MESH,
            ).start()
            return carry

        lax.fori_loop(1, yc_n, one, 0)
        mid[:, slot] = src_of(0)[...]

    def cross_copy(dx):
        return pltpu.make_async_remote_copy(
            src_ref=mid.at[dx],
            dst_ref=left.at[pl.ds(mid_low, mid_n), my_rows],
            send_sem=cross_send.at[dx - 1],
            recv_sem=cross_recv.at[dx - 1],
            device_id=(me, lays[dx]),
            device_id_type=MESH,
        )

    def first_picks(r, d, put):
        for dx in range(4):
            put(dx, gathered[r][srows[r, lays[dx], 0, d]])

    lane_q = lax.broadcasted_iota(jnp.int32, (quarter, width), 1) // quarter

    def swap(a, b, groups):
        w = groups * quarter
        low = (lane_q // groups) % 2 == 0
        return (
            jnp.where(low, a, pltpu.roll(b, w, 1)),
            jnp.where(low, pltpu.roll(a, width - w, 1), b),
        )

    backs = [lax.rem(q - lay + 4, 4) for q in range(4)]

    def left_picks(r, d, put):
        p0, p1, p2, p3 = [
            gathered[r][srows[r, j, 0, HALF + d]].astype(F32) for j in range(4)
        ]
        t0, t2 = swap(p0, p2, 2)
        t1, t3 = swap(p1, p3, 2)
        q0, q1 = swap(t0, t1, 1)
        q2, q3 = swap(t2, t3, 1)
        for q, piece in enumerate((q0, q1, q2, q3)):
            put(backs[q], piece.astype(BF))

    def fill_group(picks, dst, k):
        low, count = group(k)

        def one(m, carry):
            d = zs[0] + mate_yc(m)
            for r in range(low, low + count):

                def put(dx, value):
                    dst[m * 4 + dx, r] = value

                picks(r, d, put)
            return carry

        lax.fori_loop(0, yc_n, one, 0)

    whole_steps = list(range(1, half_z - reach))
    far_n = 2 * len(whole_steps) + 1
    far_low = 2 * reach + 1
    last_step = half_z - reach

    def far_parts():
        out = [(last_step, 0)]
        for e in whole_steps:
            out += [(e, 0), (e, 1)]
        return out

    def fill_far(picks, dst, seg):
        e, h = far_parts()[seg]
        for up in (True, False):
            r = slot_order(-reach if up else reach, z_n)
            which = 0 if up else 1
            span = h if e < last_step else which

            def one(m, carry):
                d = zs[(e if up else -e) % z_n] + mate_yc(m)

                def put(dx, value):
                    dst[which, e - 1, m * 4 + dx] = value

                picks(r, d, put)
                return carry

            lax.fori_loop(span * (yc_n // 2), (span + 1) * (yc_n // 2), one, 0)

    def far_copy(src, dst, kind, up, seg):
        e, h = far_parts()[seg]
        which = 0 if up else 1
        span = pl.ds((h if e < last_step else which) * half_plane, half_plane)
        slot = slot_order(-(reach + e) if up else reach + e, z_n) - far_low
        return pltpu.make_async_remote_copy(
            src_ref=src.at[which, e - 1, span],
            dst_ref=dst.at[slot, span],
            send_sem=far_send.at[kind, which, seg],
            recv_sem=far_recv.at[kind, which, seg],
            device_id=at_z(e if up else -e),
            device_id_type=MESH,
        )

    def far_plane_send(src, dst, which, low, count, m_low, m_high):
        def one(i, d, to):
            piece = src.at[pl.ds(low, count), i]
            plane_copy(piece, dst, which, far_low + low, count, d, to).start()

        each_mate(m_low, m_high, one)
        if m_low == 0:
            dst[pl.ds(yc * z_n + far_low + low, count), my_rows] = src[pl.ds(low, count), 0]

    def arrive(k):
        for up, s in hops():
            hop(up, k, s).wait_recv()
            if k < reach:
                hop(up, k + 1, s).start()

    both = (True, False)
    parts = range(len(far_parts()))
    for k in range(0, reach + 1):
        if k > 0:
            arrive(k)
        if k == reach:
            for seg in parts:
                fill_far(first_picks, far_out, seg)
                for up in both:
                    far_copy(far_out, far_in, 0, up, seg).start()
        fill_group(first_picks, stage, k)
        plane_send(stage, first, 0, k)
        fill_group(left_picks, lstage, k)
        if k < reach:
            left_direct(k)
    for seg in parts:
        fill_far(left_picks, lfar_out, seg)
    for seg in parts:
        for up in both:
            far_copy(far_out, far_in, 0, up, seg).wait_recv()
        if seg == 0:
            far_plane_send(far_in, first, 0, far_n - 1, 1, 0, yc_n)
        else:
            e, h = far_parts()[seg]
            half = yc_n // 2
            far_plane_send(far_in, first, 0, 2 * e - 2, 2, h * half, (h + 1) * half)
    for seg in parts:
        for up in both:
            far_copy(lfar_out, lfar_in, 1, up, seg).start()
    near_pieces = 2 * reach - 1
    mid_low = near_pieces * yc_n
    mid_n = grid_n - mid_low
    for r in (0, 1):
        left_across(r, lambda m, r=r: lstage.at[pl.ds(m * 4, 4), near_pieces + r])

    def wait_all(src, sem):
        whole = src.at[pl.ds(1, src.shape[0] - 1)]
        pltpu.make_async_copy(whole, whole, sem).wait()

    def wait_plane(dst, sem):
        whole = dst.at[pl.ds(0, (plane_n - 1) * z_n // 4)]
        pltpu.make_async_copy(whole, whole, sem).wait()

    wait_plane(first, recv_sem.at[0])

    right_lay, left_lay, far_lay = lays[1], lays[3], lays[2]

    def rows_of(q, h):
        return pl.ds(pl.multiple_of(q * quarter + h * ROWS, ROWS), ROWS)

    def reduce_rows(phase, together, product, src, got, comb, between, finish):
        def copy(kind, c):
            span = pl.ds(c * per, per)
            if kind == 0:
                ref, to = src.at[span, rows_of(far_lay, 0)], right_lay
            elif kind == 1:
                ref, to = src.at[span, rows_of(far_lay, 1)], left_lay
            elif kind == 2:
                ref, to = src.at[span, rows_of(right_lay, 1)], right_lay
            elif kind == 3:
                ref, to = src.at[span, rows_of(left_lay, 0)], left_lay
            elif kind == 4:
                ref, to = comb.at[0, span], right_lay
            else:
                ref, to = comb.at[1, span], left_lay
            return pltpu.make_async_remote_copy(
                src_ref=ref,
                dst_ref=got.at[kind, span],
                send_sem=rs_send.at[phase, kind, c],
                recv_sem=rs_recv.at[phase, kind, c],
                device_id=(me, to),
                device_id_type=MESH,
            )

        def relay(c):
            span = pl.ds(c * per, per)
            for kind, q in ((0, right_lay), (1, left_lay)):
                copy(kind, c).wait_recv()
                own = src[span, rows_of(q, kind)].astype(F32)
                comb[kind, span] = (own + got[kind, span].astype(F32)).astype(BF)
                copy(4 + kind, c).start()

        def chunk(c, carry):
            def some(i, inner):
                for n in range(together):
                    product(c * per + i * together + n)
                return inner

            lax.fori_loop(0, per // together, some, 0)
            for kind in range(4):
                copy(kind, c).start()

            @pl.when(c >= LAG)
            def _():
                relay(c - LAG)

            return carry

        lax.fori_loop(0, CHUNKS, chunk, 0)
        between()
        for c in range(CHUNKS - LAG, CHUNKS):
            relay(c)

        def close(c, carry):
            span = pl.ds(c * per, per)
            for h, direct, joined in ((0, 3, 4), (1, 2, 5)):
                copy(direct, c).wait_recv()
                copy(joined, c).wait_recv()
                total = (
                    src[span, rows_of(lay, h)].astype(F32)
                    + got[direct, span].astype(F32)
                    + got[joined, span].astype(F32)
                )
                finish(span, h, total)
            return carry

        lax.fori_loop(0, CHUNKS, close, 0)

        def drain(c, carry):
            for kind in range(6):
                copy(kind, c).wait_send()
            return carry

        return drain

    def product_first(o):
        acc = jnp.zeros((width, width), F32)
        for t in range(0, terms, 2):
            a = jnp.concatenate([first[sftab[u, 0, o]] for u in (t, t + 1)], axis=1)
            b = jnp.concatenate([first[sftab[u, 1, o]] for u in (t, t + 1)], axis=0)
            acc = acc + jnp.dot(a, b, preferred_element_type=F32)
        part[o] = acc.astype(BF)

    def finish_first(span, h, total):
        sq_ref[span, pl.ds(h * ROWS, ROWS)] = total.astype(BF)

    def send_late():
        for seg in parts:
            for up in both:
                far_copy(lfar_out, lfar_in, 1, up, seg).wait_recv()
        for f in range(far_n):
            left_across(2 + f, lambda m, f=f: lfar_in.at[f, pl.ds(m * 4, 4)])

    drain_first = reduce_rows(0, 4, product_first, part, rs1, comb1, send_late, finish_first)

    def fill_right(i, d):
        rstage[i] = sq_ref[ssr[0, d]]

    rstage[0] = sq_ref[ssr[0, me]]
    each_peer(fill_right)
    right[me] = rstage[0]

    def send_right(i, d):
        pltpu.make_async_remote_copy(
            src_ref=rstage.at[i],
            dst_ref=right.at[me],
            send_sem=send_sem.at[2],
            recv_sem=recv_sem.at[2],
            device_id=(d, lay),
            device_id_type=MESH,
        ).start()

    each_peer(send_right)
    def wait_mid(sem):
        whole = mid.at[:, pl.ds(0, mid_n // yc_n * (yc_n - 1))]
        pltpu.make_async_copy(whole, whole, sem).wait()

    wait_mid(recv_sem.at[3])
    for dx in (1, 2, 3):
        cross_copy(dx).start()
    left[pl.ds(mid_low, mid_n), my_rows] = mid[0]

    def wait_direct(sem):
        whole = lstage.at[pl.ds(1, plane_n - 1), pl.ds(0, near_pieces)]
        pltpu.make_async_copy(whole, whole, sem).wait()

    wait_direct(recv_sem.at[1])
    for dx in (1, 2, 3):
        cross_copy(dx).wait_recv()
    wait_all(rstage, recv_sem.at[2])

    lane = lax.broadcasted_iota(jnp.int32, (width, width), 1) // quarter

    def product_second(o):
        acc = jnp.zeros((width, width), F32)
        for t in range(0, terms, 2):
            a_parts, b_parts = [], []
            for u in (t, t + 1):
                lefts = [left[stab[j, u, 0, o]] for j in range(4)]
                low = jnp.where(lane == 0, lefts[0], lefts[1])
                high = jnp.where(lane == 2, lefts[2], lefts[3])
                a_parts.append(jnp.where(lane < 2, low, high))
                b_parts += [right[stab[j, u, 1, o]] for j in range(4)]
            a = jnp.concatenate(a_parts, axis=1)
            b = jnp.concatenate(b_parts, axis=0)
            acc = acc + jnp.dot(a, b, preferred_element_type=F32)
        part2[o] = acc.astype(BF)

    def finish_second(span, h, total):
        own = x_ref[span, rows_of(lay, h)].astype(F32)
        out_ref[span, pl.ds(h * ROWS, ROWS)] = (1.5 * own - 0.5 * total).astype(BF)

    drain_second = reduce_rows(
        1, 4, product_second, part2, rs2, comb2, lambda: None, finish_second
    )

    lax.fori_loop(0, CHUNKS, drain_first, 0)
    lax.fori_loop(0, CHUNKS, drain_second, 0)
    for k in range(1, reach + 1):
        for up, s in hops():
            hop(up, k, s).wait_send()
    for step in range(1, 4):
        tab_copy(step).wait_send()
        row_copy(step).wait_send()
    for step in near:
        rows_copy(step).wait_send()
    for seg in parts:
        for up in both:
            far_copy(far_out, far_in, 0, up, seg).wait_send()
            far_copy(lfar_out, lfar_in, 1, up, seg).wait_send()
    wait_plane(first, send_sem.at[0])
    wait_direct(send_sem.at[1])
    wait_mid(send_sem.at[3])
    for dx in (1, 2, 3):
        cross_copy(dx).wait_send()
    wait_all(rstage, send_sem.at[2])


def local(
    y_n,
    x_blocks,
    send_first,
    send_left,
    send_right,
    terms_first,
    terms_second,
    live_first,
    live_second,
):
    grid_n = lax.axis_size("grid")
    blocks, width = x_blocks.shape[0], x_blocks.shape[1]
    count = terms_first.shape[2]
    quarter = width // 4
    yc_n = 2 * y_n
    z_n = grid_n // yc_n

    reach = z_n // 4
    steps = z_n // 2 - reach
    near_n = 2 * reach + 1

    def by_term(table):
        return table.reshape(blocks, count, 2).transpose(1, 2, 0)

    small = (
        send_first.reshape(1, grid_n),
        send_left.reshape(1, grid_n),
        send_right.reshape(1, grid_n),
        by_term(terms_first),
        by_term(terms_second),
        live_first.reshape(1, blocks),
        live_second.reshape(1, blocks),
    )
    share = jax.ShapeDtypeStruct((blocks, quarter, width), BF)
    vmem = pl.BlockSpec(memory_space=pltpu.VMEM)
    smem = pl.BlockSpec(memory_space=pltpu.SMEM)
    dma = pltpu.SemaphoreType.DMA
    return pl.pallas_call(
        functools.partial(kernel, grid_n, y_n, blocks, count),
        out_shape=(share, share),
        in_specs=[pl.BlockSpec(memory_space=pl.ANY), vmem, vmem, smem, vmem, vmem, vmem, vmem],
        out_specs=(vmem, vmem),
        scratch_shapes=[
            pltpu.VMEM((blocks, width, width), BF),
            *[pltpu.VMEM((blocks, quarter, width), BF)] * near_n,
            pltpu.VMEM((yc_n * 4, near_n, quarter, width), BF),
            pltpu.VMEM((yc_n * 4, near_n, quarter, width), BF),
            pltpu.VMEM((2, steps, yc_n * 4, quarter, width), BF),
            pltpu.VMEM((z_n - near_n, yc_n * 4, quarter, width), BF),
            pltpu.VMEM((2, steps, yc_n * 4, quarter, width), BF),
            pltpu.VMEM((z_n - near_n, yc_n * 4, quarter, width), BF),
            pltpu.VMEM((4, grid_n - (2 * reach - 1) * yc_n, quarter, width), BF),
            pltpu.VMEM((grid_n, quarter, width), BF),
            pltpu.VMEM((grid_n + 1, width, width), BF),
            pltpu.VMEM((grid_n + 1, width, width), BF),
            pltpu.VMEM((grid_n, quarter, width), BF),
            pltpu.VMEM((blocks, width, width), BF),
            pltpu.VMEM((blocks, width, width), BF),
            pltpu.VMEM((6, blocks, ROWS, width), BF),
            pltpu.VMEM((6, blocks, ROWS, width), BF),
            pltpu.VMEM((2, blocks, ROWS, width), BF),
            pltpu.VMEM((2, blocks, ROWS, width), BF),
            pltpu.VMEM((count, 2, 128), jnp.int32),
            pltpu.SMEM((count, 2, 128), jnp.int32),
            pltpu.VMEM((4, count, 2, 128), jnp.int32),
            pltpu.SMEM((4, count, 2, 128), jnp.int32),
            pltpu.VMEM((near_n, 4, 1, 128), jnp.int32),
            pltpu.SMEM((near_n, 4, 1, 128), jnp.int32),
            dma((4,)),
            dma((4,)),
            dma((2, reach, SUBS)),
            dma((2, reach, SUBS)),
            dma((2, 2, 2 * steps - 1)),
            dma((2, 2, 2 * steps - 1)),
            dma((3,)),
            dma((3,)),
            dma((3,)),
            dma((3,)),
            dma((2 + z_n,)),
            dma((2 + z_n,)),
            dma((3,)),
            dma((2, 6, CHUNKS)),
            dma((2, 6, CHUNKS)),
        ],
        compiler_params=pltpu.CompilerParams(
            collective_id=0, has_side_effects=True, vmem_limit_bytes=60 * 1024 * 1024
        ),
    )(x_blocks, *small)


def solution(mesh, y_n=4):
    return jax.shard_map(
        functools.partial(local, y_n),
        mesh=mesh,
        in_specs=(
            P("grid", None, None),
            P("grid", "layer", None, None),
            P("grid", "layer", None, None),
            P("grid", None, None),
            P("grid", "layer", None, None),
            P("grid", "layer", None, None),
            P("grid", "layer"),
            P("grid", "layer"),
        ),
        out_specs=(P("grid", "layer", None), P("grid", "layer", None)),
        check_vma=False,
    )
```

```python
import functools

import jax
import jax.numpy as jnp
from jax import lax
from jax.experimental import pallas as pl
from jax.experimental.pallas import tpu as pltpu
from jax.sharding import PartitionSpec as P

MESH = pl.DeviceIdType.MESH
BF = jnp.bfloat16
F32 = jnp.float32
HALF = 64
CHUNKS = 8
LAG = 2
DIRECT = 1
FAR_FIRST = (4, 3, 5, 2, 6, 1, 7)
ROWS = 16
SUBS = 2


def slot_order(k, n):
    k = k % n
    return 0 if k == 0 else (2 * k - 1 if 2 * k <= n else 2 * (n - k))


def kernel(
    grid_n,
    y_n,
    blocks,
    terms,
    x_hbm,
    sf_ref,
    sl_ref,
    ssr,
    tf_ref,
    ts_ref,
    lf_ref,
    ls_ref,
    sq_ref,
    out_ref,
    x_ref,
    *refs,
):
    near_n = 2 * (grid_n // (2 * y_n) // 4) + 1
    gathered = refs[:near_n]
    run(
        grid_n, y_n, blocks, terms, x_hbm, sf_ref, sl_ref, ssr, tf_ref, ts_ref, lf_ref, ls_ref,
        sq_ref, out_ref, x_ref, gathered, *refs[near_n:]
    )


def run(
    grid_n,
    y_n,
    blocks,
    terms,
    x_hbm,
    sf_ref,
    sl_ref,
    ssr,
    tf_ref,
    ts_ref,
    lf_ref,
    ls_ref,
    sq_ref,
    out_ref,
    x_ref,
    gathered,
    stage,
    lstage,
    far_out,
    far_in,
    lfar_out,
    lfar_in,
    mid,
    rstage,
    first,
    left,
    right,
    part,
    part2,
    rs1,
    rs2,
    comb1,
    comb2,
    ftab,
    sftab,
    tabs,
    stab,
    rows,
    srows,
    send_sem,
    recv_sem,
    ring_send,
    ring_recv,
    far_send,
    far_recv,
    cross_send,
    cross_recv,
    tab_send,
    tab_recv,
    row_send,
    row_recv,
    loc_sem,
    rs_send,
    rs_recv,
):
    me = lax.axis_index("grid")
    lay = lax.axis_index("layer")
    load_x = pltpu.make_async_copy(x_hbm, x_ref, loc_sem.at[0])
    load_x.start()
    width = x_ref.shape[1]
    quarter = width // 4
    z_n = grid_n // (2 * y_n)
    yc_n = 2 * y_n
    z, y, core = me // yc_n, (me // 2) % y_n, me % 2
    yc = y * 2 + core
    per = blocks // CHUNKS
    sub = blocks // SUBS
    plane_n = yc_n * 4
    half_z = z_n // 2
    reach = half_z // 2
    half_plane = plane_n // 2
    zs = [lax.rem(z + dz, z_n) * yc_n for dz in range(z_n)]
    lays = [lax.rem(lay + dx, 4) for dx in range(4)]

    def mate_yc(m):
        return lax.rem(y + lax.div(m, 2), y_n) * 2 + lax.rem(core + m, 2)

    def at_z(dz):
        return (zs[dz % z_n] + yc, lay)

    def each_peer(act):
        def one(m, carry):
            other = mate_yc(m)
            for dz in FAR_FIRST:
                if 0 < dz < z_n:
                    act(m * z_n + dz, zs[dz] + other)

            @pl.when(m > 0)
            def _():
                act(m * z_n, zs[0] + other)

            return carry

        lax.fori_loop(0, yc_n, one, 0)

    def each_mate(low, high, act):
        def one(m, carry):
            d = zs[0] + mate_yc(m)
            for dx in range(1, 4):
                act(m * 4 + dx, d, lays[dx])

            @pl.when(m > 0)
            def _():
                act(m * 4, d, lay)

            return carry

        lax.fori_loop(low, high, one, 0)

    my_rows = pl.ds(pl.multiple_of(lay * quarter, quarter), quarter)

    barrier = pltpu.get_barrier_semaphore()

    def greet(d, to):
        pl.semaphore_signal(barrier, inc=1, device_id=(d, to), device_id_type=MESH)

    each_peer(lambda i, d: greet(d, lay))

    def greet_layers(m, carry):
        d = zs[0] + mate_yc(m)
        for dx in range(1, 4):
            greet(d, lays[dx])
        return carry

    lax.fori_loop(0, yc_n, greet_layers, 0)

    def moved(slots):
        away = lax.rem(lax.div(slots, yc_n) - z + z_n, z_n)
        order = jnp.where(2 * away <= z_n, 2 * away - 1, 2 * (z_n - away))
        order = jnp.where(away == 0, 0, order)
        return lax.rem(slots, yc_n), order

    def pad_row(values):
        return jnp.pad(values, ((0, 0), (0, HALF - values.shape[1])))

    term = lax.broadcasted_iota(jnp.int32, (terms, 1, blocks), 0)
    span_o = pl.ds(0, blocks)
    for table, live, to in ((tf_ref, lf_ref, ftab), (ts_ref, ls_ref, tabs.at[lay])):
        keep = term < live[...].reshape(1, 1, blocks)
        to[...] = jnp.zeros(to.shape, jnp.int32)
        lefts, rights = table[:, pl.ds(0, 1)], table[:, pl.ds(1, 1)]
        at_yc, order = moved(lefts)
        if to is ftab:
            lefts = at_yc * z_n + order
            at_yc, order = moved(rights)
            rights = at_yc * z_n + order
        else:
            lefts = order * yc_n + at_yc
        to[:, pl.ds(0, 1), span_o] = jnp.where(keep, lefts, grid_n)
        to[:, pl.ds(1, 1), span_o] = rights
    rows[0, lay] = jnp.concatenate([pad_row(sf_ref[...]), pad_row(sl_ref[...])], axis=1)
    first[grid_n] = jnp.zeros((width, width), BF)
    left[grid_n] = jnp.zeros((width, width), BF)
    load_x.wait()
    gathered[0][...] = x_ref[:, my_rows, :]
    pl.semaphore_wait(barrier, grid_n - 1 + 3 * yc_n)

    def hop(up, k, s):
        if k == 1:
            src = 0
        else:
            src = slot_order(-(k - 1) if up else k - 1, z_n)
        dst = slot_order(-k if up else k, z_n)
        span = pl.ds(s * sub, sub)
        which = 0 if up else 1
        return pltpu.make_async_remote_copy(
            src_ref=gathered[src].at[span],
            dst_ref=gathered[dst].at[span],
            send_sem=ring_send.at[which, k - 1, s],
            recv_sem=ring_recv.at[which, k - 1, s],
            device_id=at_z(1 if up else -1),
            device_id_type=MESH,
        )

    def hops():
        return [(up, s) for s in range(SUBS) for up in (True, False)]

    def tab_copy(step):
        return pltpu.make_async_remote_copy(
            src_ref=tabs.at[lay],
            dst_ref=tabs.at[lay],
            send_sem=tab_send.at[step - 1],
            recv_sem=tab_recv.at[step - 1],
            device_id=(me, lays[step]),
            device_id_type=MESH,
        )

    def row_copy(step):
        return pltpu.make_async_remote_copy(
            src_ref=rows.at[0, lay],
            dst_ref=rows.at[0, lay],
            send_sem=row_send.at[step - 1],
            recv_sem=row_recv.at[step - 1],
            device_id=(me, lays[step]),
            device_id_type=MESH,
        )

    def rows_copy(step):
        return pltpu.make_async_remote_copy(
            src_ref=rows.at[0],
            dst_ref=rows.at[slot_order(-step, z_n)],
            send_sem=row_send.at[2 + step % z_n],
            recv_sem=row_recv.at[2 + step % z_n],
            device_id=at_z(step),
            device_id_type=MESH,
        )

    for step in range(1, 4):
        row_copy(step).start()
    for up, s in hops():
        hop(up, 1, s).start()
    for step in range(1, 4):
        tab_copy(step).start()
    for step in range(1, 4):
        row_copy(step).wait_recv()
    near = [step for k in range(1, reach + 1) for step in (k, -k)]
    for step in near:
        rows_copy(step).start()
    for step in near:
        rows_copy(step).wait_recv()
    for step in range(1, 4):
        tab_copy(step).wait_recv()
    moves = [
        pltpu.make_async_copy(rows, srows, loc_sem.at[0]),
        pltpu.make_async_copy(tabs, stab, loc_sem.at[1]),
        pltpu.make_async_copy(ftab, sftab, loc_sem.at[2]),
    ]
    for move in moves:
        move.start()
    for move in moves:
        move.wait()

    def group(k):
        if k == 0:
            return 0, 1
        return 2 * k - 1, 2

    def plane_copy(src, dst, which, low, count, d, to):
        return pltpu.make_async_remote_copy(
            src_ref=src,
            dst_ref=dst.at[pl.ds(yc * z_n + low, count), my_rows],
            send_sem=send_sem.at[which],
            recv_sem=recv_sem.at[which],
            device_id=(d, to),
            device_id_type=MESH,
        )

    def plane_send(src, dst, which, k):
        low, count = group(k)

        def one(i, d, to):
            plane_copy(src.at[i, pl.ds(low, count)], dst, which, low, count, d, to).start()

        each_mate(0, yc_n, one)
        dst[pl.ds(yc * z_n + low, count), my_rows] = src[0, pl.ds(low, count)]

    def left_direct(pieces):
        for r in pieces:
            slots = pl.ds(r * yc_n + yc, 1)

            def one(i, d, to):
                pltpu.make_async_remote_copy(
                    src_ref=lstage.at[i, pl.ds(r, 1)],
                    dst_ref=left.at[slots, my_rows],
                    send_sem=send_sem.at[1],
                    recv_sem=recv_sem.at[1],
                    device_id=(d, to),
                    device_id_type=MESH,
                ).start()

            each_mate(0, yc_n, one)
            left[slots, my_rows] = lstage[0, pl.ds(r, 1)]

    def left_across(piece, src_of):
        slot = piece * yc_n + yc

        def one(m, carry):
            pltpu.make_async_remote_copy(
                src_ref=src_of(m),
                dst_ref=mid.at[:, slot],
                send_sem=send_sem.at[3],
                recv_sem=recv_sem.at[3],
                device_id=(zs[0] + mate_yc(m), lay),
                device_id_type=MESH,
            ).start()
            return carry

        lax.fori_loop(1, yc_n, one, 0)
        mid[:, slot] = src_of(0)[...]

    def cross_copy(dx):
        return pltpu.make_async_remote_copy(
            src_ref=mid.at[dx],
            dst_ref=left.at[pl.ds(mid_low, mid_n), my_rows],
            send_sem=cross_send.at[dx - 1],
            recv_sem=cross_recv.at[dx - 1],
            device_id=(me, lays[dx]),
            device_id_type=MESH,
        )

    def first_picks(r, d, put):
        for dx in range(4):
            put(dx, gathered[r][srows[r, lays[dx], 0, d]])

    lane_q = lax.broadcasted_iota(jnp.int32, (quarter, width), 1) // quarter

    def swap(a, b, groups):
        w = groups * quarter
        low = (lane_q // groups) % 2 == 0
        return (
            jnp.where(low, a, pltpu.roll(b, w, 1)),
            jnp.where(low, pltpu.roll(a, width - w, 1), b),
        )

    backs = [lax.rem(q - lay + 4, 4) for q in range(4)]

    def left_picks(r, d, put):
        p0, p1, p2, p3 = [
            gathered[r][srows[r, j, 0, HALF + d]].astype(F32) for j in range(4)
        ]
        t0, t2 = swap(p0, p2, 2)
        t1, t3 = swap(p1, p3, 2)
        q0, q1 = swap(t0, t1, 1)
        q2, q3 = swap(t2, t3, 1)
        for q, piece in enumerate((q0, q1, q2, q3)):
            put(backs[q], piece.astype(BF))

    def fill_group(picks, dst, k):
        low, count = group(k)

        def one(m, carry):
            d = zs[0] + mate_yc(m)
            for r in range(low, low + count):

                def put(dx, value):
                    dst[m * 4 + dx, r] = value

                picks(r, d, put)
            return carry

        lax.fori_loop(0, yc_n, one, 0)

    whole_steps = list(range(1, half_z - reach))
    far_n = 2 * len(whole_steps) + 1
    far_low = 2 * reach + 1
    last_step = half_z - reach

    def far_parts():
        out = [(last_step, 0)]
        for e in whole_steps:
            out += [(e, 0), (e, 1)]
        return out

    def fill_far(picks, dst, seg):
        e, h = far_parts()[seg]
        for up in (True, False):
            r = slot_order(-reach if up else reach, z_n)
            which = 0 if up else 1
            span = h if e < last_step else which

            def one(m, carry):
                d = zs[(e if up else -e) % z_n] + mate_yc(m)

                def put(dx, value):
                    dst[which, e - 1, m * 4 + dx] = value

                picks(r, d, put)
                return carry

            lax.fori_loop(span * (yc_n // 2), (span + 1) * (yc_n // 2), one, 0)

    def far_copy(src, dst, kind, up, seg):
        e, h = far_parts()[seg]
        which = 0 if up else 1
        span = pl.ds((h if e < last_step else which) * half_plane, half_plane)
        slot = slot_order(-(reach + e) if up else reach + e, z_n) - far_low
        return pltpu.make_async_remote_copy(
            src_ref=src.at[which, e - 1, span],
            dst_ref=dst.at[slot, span],
            send_sem=far_send.at[kind, which, seg],
            recv_sem=far_recv.at[kind, which, seg],
            device_id=at_z(e if up else -e),
            device_id_type=MESH,
        )

    def far_plane_send(src, dst, which, low, count, m_low, m_high):
        def one(i, d, to):
            piece = src.at[pl.ds(low, count), i]
            plane_copy(piece, dst, which, far_low + low, count, d, to).start()

        each_mate(m_low, m_high, one)
        if m_low == 0:
            dst[pl.ds(yc * z_n + far_low + low, count), my_rows] = src[pl.ds(low, count), 0]

    def arrive(k):
        for up, s in hops():
            hop(up, k, s).wait_recv()
            if k < reach:
                hop(up, k + 1, s).start()

    both = (True, False)
    parts = range(len(far_parts()))
    for k in range(0, reach + 1):
        if k > 0:
            arrive(k)
        if k == reach:
            for seg in parts:
                fill_far(first_picks, far_out, seg)
                for up in both:
                    far_copy(far_out, far_in, 0, up, seg).start()
        fill_group(first_picks, stage, k)
        plane_send(stage, first, 0, k)
        fill_group(left_picks, lstage, k)
        if k < reach:
            low, count = group(k)
            left_direct(range(low, low + count))
    for seg in parts:
        fill_far(left_picks, lfar_out, seg)
    for seg in parts:
        for up in both:
            far_copy(far_out, far_in, 0, up, seg).wait_recv()
        if seg == 0:
            far_plane_send(far_in, first, 0, far_n - 1, 1, 0, yc_n)
        else:
            e, h = far_parts()[seg]
            half = yc_n // 2
            far_plane_send(far_in, first, 0, 2 * e - 2, 2, h * half, (h + 1) * half)
    for seg in parts:
        for up in both:
            far_copy(lfar_out, lfar_in, 1, up, seg).start()
    near_pieces = 2 * reach - 1 + DIRECT
    mid_low = near_pieces * yc_n
    mid_n = grid_n - mid_low
    left_direct(range(2 * reach - 1, near_pieces))
    for r in range(2 - DIRECT):
        left_across(r, lambda m, r=r: lstage.at[pl.ds(m * 4, 4), near_pieces + r])

    def wait_all(src, sem):
        whole = src.at[pl.ds(1, src.shape[0] - 1)]
        pltpu.make_async_copy(whole, whole, sem).wait()

    def wait_plane(dst, sem):
        whole = dst.at[pl.ds(0, (plane_n - 1) * z_n // 4)]
        pltpu.make_async_copy(whole, whole, sem).wait()

    wait_plane(first, recv_sem.at[0])

    right_lay, left_lay, far_lay = lays[1], lays[3], lays[2]

    def rows_of(q, h):
        return pl.ds(pl.multiple_of(q * quarter + h * ROWS, ROWS), ROWS)

    def reduce_rows(phase, together, product, src, got, comb, midway, between, finish):
        def copy(kind, c):
            span = pl.ds(c * per, per)
            if kind == 0:
                ref, to = src.at[span, rows_of(far_lay, 0)], right_lay
            elif kind == 1:
                ref, to = src.at[span, rows_of(far_lay, 1)], left_lay
            elif kind == 2:
                ref, to = src.at[span, rows_of(right_lay, 1)], right_lay
            elif kind == 3:
                ref, to = src.at[span, rows_of(left_lay, 0)], left_lay
            elif kind == 4:
                ref, to = comb.at[0, span], right_lay
            else:
                ref, to = comb.at[1, span], left_lay
            return pltpu.make_async_remote_copy(
                src_ref=ref,
                dst_ref=got.at[kind, span],
                send_sem=rs_send.at[phase, kind, c],
                recv_sem=rs_recv.at[phase, kind, c],
                device_id=(me, to),
                device_id_type=MESH,
            )

        def relay(c):
            span = pl.ds(c * per, per)
            for kind, q in ((0, right_lay), (1, left_lay)):
                copy(kind, c).wait_recv()
                own = src[span, rows_of(q, kind)].astype(F32)
                comb[kind, span] = (own + got[kind, span].astype(F32)).astype(BF)
                copy(4 + kind, c).start()

        def chunk(c, carry):
            def some(i, inner):
                for n in range(together):
                    product(c * per + i * together + n)
                return inner

            lax.fori_loop(0, per // together, some, 0)
            for kind in range(4):
                copy(kind, c).start()

            @pl.when(c >= LAG)
            def _():
                relay(c - LAG)

            @pl.when(c == CHUNKS // 2 - 1)
            def _():
                midway()

            return carry

        lax.fori_loop(0, CHUNKS, chunk, 0)
        for c in range(CHUNKS - LAG, CHUNKS):
            relay(c)
        between()

        def close(c, carry):
            span = pl.ds(c * per, per)
            for h, direct, joined in ((0, 3, 4), (1, 2, 5)):
                copy(direct, c).wait_recv()
                copy(joined, c).wait_recv()
                total = (
                    src[span, rows_of(lay, h)].astype(F32)
                    + got[direct, span].astype(F32)
                    + got[joined, span].astype(F32)
                )
                finish(span, h, total)
            return carry

        lax.fori_loop(0, CHUNKS, close, 0)

        def drain(c, carry):
            for kind in range(6):
                copy(kind, c).wait_send()
            return carry

        return drain

    def product_first(o):
        acc = jnp.zeros((width, width), F32)
        for t in range(0, terms, 2):
            a = jnp.concatenate([first[sftab[u, 0, o]] for u in (t, t + 1)], axis=1)
            b = jnp.concatenate([first[sftab[u, 1, o]] for u in (t, t + 1)], axis=0)
            acc = acc + jnp.dot(a, b, preferred_element_type=F32)
        part[o] = acc.astype(BF)

    def finish_first(span, h, total):
        sq_ref[span, pl.ds(h * ROWS, ROWS)] = total.astype(BF)

    def send_late():
        for seg in parts:
            for up in both:
                far_copy(lfar_out, lfar_in, 1, up, seg).wait_recv()
        for f in range(far_n):
            left_across(2 - DIRECT + f, lambda m, f=f: lfar_in.at[f, pl.ds(m * 4, 4)])

    def wait_mid(sem):
        whole = mid.at[:, pl.ds(0, mid_n // yc_n * (yc_n - 1))]
        pltpu.make_async_copy(whole, whole, sem).wait()

    def send_cross():
        wait_mid(recv_sem.at[3])
        for dx in (1, 2, 3):
            cross_copy(dx).start()

    drain_first = reduce_rows(
        0, 4, product_first, part, rs1, comb1, send_late, lambda: None, finish_first
    )

    def fill_right(i, d):
        rstage[i] = sq_ref[ssr[0, d]]

    rstage[0] = sq_ref[ssr[0, me]]
    each_peer(fill_right)
    right[me] = rstage[0]

    def send_right(i, d):
        pltpu.make_async_remote_copy(
            src_ref=rstage.at[i],
            dst_ref=right.at[me],
            send_sem=send_sem.at[2],
            recv_sem=recv_sem.at[2],
            device_id=(d, lay),
            device_id_type=MESH,
        ).start()

    each_peer(send_right)
    send_cross()
    left[pl.ds(mid_low, mid_n), my_rows] = mid[0]

    def wait_direct(sem):
        whole = lstage.at[pl.ds(1, plane_n - 1), pl.ds(0, near_pieces)]
        pltpu.make_async_copy(whole, whole, sem).wait()

    wait_direct(recv_sem.at[1])
    for dx in (1, 2, 3):
        cross_copy(dx).wait_recv()
    wait_all(rstage, recv_sem.at[2])

    lane = lax.broadcasted_iota(jnp.int32, (width, width), 1) // quarter

    def product_second(o):
        acc = jnp.zeros((width, width), F32)
        for t in range(0, terms, 2):
            a_parts, b_parts = [], []
            for u in (t, t + 1):
                lefts = [left[stab[j, u, 0, o]] for j in range(4)]
                low = jnp.where(lane == 0, lefts[0], lefts[1])
                high = jnp.where(lane == 2, lefts[2], lefts[3])
                a_parts.append(jnp.where(lane < 2, low, high))
                b_parts += [right[stab[j, u, 1, o]] for j in range(4)]
            a = jnp.concatenate(a_parts, axis=1)
            b = jnp.concatenate(b_parts, axis=0)
            acc = acc + jnp.dot(a, b, preferred_element_type=F32)
        part2[o] = acc.astype(BF)

    def finish_second(span, h, total):
        own = x_ref[span, rows_of(lay, h)].astype(F32)
        out_ref[span, pl.ds(h * ROWS, ROWS)] = (1.5 * own - 0.5 * total).astype(BF)

    drain_second = reduce_rows(
        1, 4, product_second, part2, rs2, comb2, lambda: None, lambda: None, finish_second
    )

    lax.fori_loop(0, CHUNKS, drain_first, 0)
    lax.fori_loop(0, CHUNKS, drain_second, 0)
    for k in range(1, reach + 1):
        for up, s in hops():
            hop(up, k, s).wait_send()
    for step in range(1, 4):
        tab_copy(step).wait_send()
        row_copy(step).wait_send()
    for step in near:
        rows_copy(step).wait_send()
    for seg in parts:
        for up in both:
            far_copy(far_out, far_in, 0, up, seg).wait_send()
            far_copy(lfar_out, lfar_in, 1, up, seg).wait_send()
    wait_plane(first, send_sem.at[0])
    wait_direct(send_sem.at[1])
    wait_mid(send_sem.at[3])
    for dx in (1, 2, 3):
        cross_copy(dx).wait_send()
    wait_all(rstage, send_sem.at[2])


def local(
    y_n,
    x_blocks,
    send_first,
    send_left,
    send_right,
    terms_first,
    terms_second,
    live_first,
    live_second,
):
    grid_n = lax.axis_size("grid")
    blocks, width = x_blocks.shape[0], x_blocks.shape[1]
    count = terms_first.shape[2]
    quarter = width // 4
    yc_n = 2 * y_n
    z_n = grid_n // yc_n

    reach = z_n // 4
    steps = z_n // 2 - reach
    near_n = 2 * reach + 1

    def by_term(table):
        return table.reshape(blocks, count, 2).transpose(1, 2, 0)

    small = (
        send_first.reshape(1, grid_n),
        send_left.reshape(1, grid_n),
        send_right.reshape(1, grid_n),
        by_term(terms_first),
        by_term(terms_second),
        live_first.reshape(1, blocks),
        live_second.reshape(1, blocks),
    )
    share = jax.ShapeDtypeStruct((blocks, quarter, width), BF)
    vmem = pl.BlockSpec(memory_space=pltpu.VMEM)
    smem = pl.BlockSpec(memory_space=pltpu.SMEM)
    dma = pltpu.SemaphoreType.DMA
    return pl.pallas_call(
        functools.partial(kernel, grid_n, y_n, blocks, count),
        out_shape=(share, share),
        in_specs=[pl.BlockSpec(memory_space=pl.ANY), vmem, vmem, smem, vmem, vmem, vmem, vmem],
        out_specs=(vmem, vmem),
        scratch_shapes=[
            pltpu.VMEM((blocks, width, width), BF),
            *[pltpu.VMEM((blocks, quarter, width), BF)] * near_n,
            pltpu.VMEM((yc_n * 4, near_n, quarter, width), BF),
            pltpu.VMEM((yc_n * 4, near_n, quarter, width), BF),
            pltpu.VMEM((2, steps, yc_n * 4, quarter, width), BF),
            pltpu.VMEM((z_n - near_n, yc_n * 4, quarter, width), BF),
            pltpu.VMEM((2, steps, yc_n * 4, quarter, width), BF),
            pltpu.VMEM((z_n - near_n, yc_n * 4, quarter, width), BF),
            pltpu.VMEM((4, grid_n - (2 * reach - 1 + DIRECT) * yc_n, quarter, width), BF),
            pltpu.VMEM((grid_n, quarter, width), BF),
            pltpu.VMEM((grid_n + 1, width, width), BF),
            pltpu.VMEM((grid_n + 1, width, width), BF),
            pltpu.VMEM((grid_n, quarter, width), BF),
            pltpu.VMEM((blocks, width, width), BF),
            pltpu.VMEM((blocks, width, width), BF),
            pltpu.VMEM((6, blocks, ROWS, width), BF),
            pltpu.VMEM((6, blocks, ROWS, width), BF),
            pltpu.VMEM((2, blocks, ROWS, width), BF),
            pltpu.VMEM((2, blocks, ROWS, width), BF),
            pltpu.VMEM((count, 2, 128), jnp.int32),
            pltpu.SMEM((count, 2, 128), jnp.int32),
            pltpu.VMEM((4, count, 2, 128), jnp.int32),
            pltpu.SMEM((4, count, 2, 128), jnp.int32),
            pltpu.VMEM((near_n, 4, 1, 128), jnp.int32),
            pltpu.SMEM((near_n, 4, 1, 128), jnp.int32),
            dma((4,)),
            dma((4,)),
            dma((2, reach, SUBS)),
            dma((2, reach, SUBS)),
            dma((2, 2, 2 * steps - 1)),
            dma((2, 2, 2 * steps - 1)),
            dma((3,)),
            dma((3,)),
            dma((3,)),
            dma((3,)),
            dma((2 + z_n,)),
            dma((2 + z_n,)),
            dma((3,)),
            dma((2, 6, CHUNKS)),
            dma((2, 6, CHUNKS)),
        ],
        compiler_params=pltpu.CompilerParams(
            collective_id=0, has_side_effects=True, vmem_limit_bytes=60 * 1024 * 1024
        ),
    )(x_blocks, *small)


def solution(mesh, y_n=4):
    return jax.shard_map(
        functools.partial(local, y_n),
        mesh=mesh,
        in_specs=(
            P("grid", None, None),
            P("grid", "layer", None, None),
            P("grid", "layer", None, None),
            P("grid", None, None),
            P("grid", "layer", None, None),
            P("grid", "layer", None, None),
            P("grid", "layer"),
            P("grid", "layer"),
        ),
        out_specs=(P("grid", "layer", None), P("grid", "layer", None)),
        check_vma=False,
    )
```

```python
import functools

import jax
import jax.numpy as jnp
from jax import lax
from jax.experimental import pallas as pl
from jax.experimental.pallas import tpu as pltpu
from jax.sharding import PartitionSpec as P

MESH = pl.DeviceIdType.MESH
BF = jnp.bfloat16
F32 = jnp.float32
HALF = 64
CHUNKS = 8
LAG = 2
DIRECT = 1
FAR_FIRST = (4, 3, 5, 2, 6, 1, 7)
ROWS = 16
SUBS = 2


def slot_order(k, n):
    k = k % n
    return 0 if k == 0 else (2 * k - 1 if 2 * k <= n else 2 * (n - k))


def kernel(grid_n, y_n, blocks, terms, x_hbm, *refs):
    near_n = 2 * (grid_n // (2 * y_n) // 4) + 1
    small, outs, refs = refs[:7], refs[7:9], refs[9:]
    held, x_ref, gathered, rest = refs[:7], refs[7], refs[8 : 8 + near_n], refs[8 + near_n :]
    run(grid_n, y_n, blocks, terms, x_hbm, small, *held, *outs, x_ref, gathered, *rest)


def run(
    grid_n,
    y_n,
    blocks,
    terms,
    x_hbm,
    small,
    sf_ref,
    sl_ref,
    ssr,
    tf_ref,
    ts_ref,
    lf_ref,
    ls_ref,
    sq_ref,
    out_ref,
    x_ref,
    gathered,
    stage,
    lstage,
    far_out,
    far_in,
    lfar_out,
    lfar_in,
    mid,
    rstage,
    first,
    left,
    right,
    part,
    part2,
    rs1,
    rs2,
    comb1,
    comb2,
    ftab,
    sftab,
    tabs,
    stab,
    rows,
    srows,
    send_sem,
    recv_sem,
    ring_send,
    ring_recv,
    far_send,
    far_recv,
    cross_send,
    cross_recv,
    tab_send,
    tab_recv,
    row_send,
    row_recv,
    loc_sem,
    rs_send,
    rs_recv,
):
    me = lax.axis_index("grid")
    lay = lax.axis_index("layer")
    load_x = pltpu.make_async_copy(x_hbm, x_ref, loc_sem.at[0])
    held = (sf_ref, sl_ref, ssr, tf_ref, ts_ref, lf_ref, ls_ref)
    loads = [
        pltpu.make_async_copy(src, dst, loc_sem.at[3 + n])
        for n, (src, dst) in enumerate(zip(small, held))
    ]
    for load in (*loads, load_x):
        load.start()
    width = x_ref.shape[1]
    quarter = width // 4
    z_n = grid_n // (2 * y_n)
    yc_n = 2 * y_n
    z, y, core = me // yc_n, (me // 2) % y_n, me % 2
    yc = y * 2 + core
    per = blocks // CHUNKS
    sub = blocks // SUBS
    plane_n = yc_n * 4
    half_z = z_n // 2
    reach = half_z // 2
    half_plane = plane_n // 2
    zs = [lax.rem(z + dz, z_n) * yc_n for dz in range(z_n)]
    lays = [lax.rem(lay + dx, 4) for dx in range(4)]

    def mate_yc(m):
        return lax.rem(y + lax.div(m, 2), y_n) * 2 + lax.rem(core + m, 2)

    def at_z(dz):
        return (zs[dz % z_n] + yc, lay)

    def each_peer(act):
        def one(m, carry):
            other = mate_yc(m)
            for dz in FAR_FIRST:
                if 0 < dz < z_n:
                    act(m * z_n + dz, zs[dz] + other)

            @pl.when(m > 0)
            def _():
                act(m * z_n, zs[0] + other)

            return carry

        lax.fori_loop(0, yc_n, one, 0)

    def each_mate(low, high, act):
        def one(m, carry):
            d = zs[0] + mate_yc(m)
            for dx in range(1, 4):
                act(m * 4 + dx, d, lays[dx])

            @pl.when(m > 0)
            def _():
                act(m * 4, d, lay)

            return carry

        lax.fori_loop(low, high, one, 0)

    my_rows = pl.ds(pl.multiple_of(lay * quarter, quarter), quarter)

    barrier = pltpu.get_barrier_semaphore()

    def greet(d, to):
        pl.semaphore_signal(barrier, inc=1, device_id=(d, to), device_id_type=MESH)

    each_peer(lambda i, d: greet(d, lay))

    def greet_layers(m, carry):
        d = zs[0] + mate_yc(m)
        for dx in range(1, 4):
            greet(d, lays[dx])
        return carry

    lax.fori_loop(0, yc_n, greet_layers, 0)
    for load in loads:
        load.wait()

    def moved(slots):
        away = lax.rem(lax.div(slots, yc_n) - z + z_n, z_n)
        order = jnp.where(2 * away <= z_n, 2 * away - 1, 2 * (z_n - away))
        order = jnp.where(away == 0, 0, order)
        return lax.rem(slots, yc_n), order

    def pad_row(values):
        return jnp.pad(values, ((0, 0), (0, HALF - values.shape[1])))

    term = lax.broadcasted_iota(jnp.int32, (terms, 1, blocks), 0)
    span_o = pl.ds(0, blocks)
    for table, live, to in ((tf_ref, lf_ref, ftab), (ts_ref, ls_ref, tabs.at[lay])):
        keep = term < live[...].reshape(1, 1, blocks)
        to[...] = jnp.zeros(to.shape, jnp.int32)
        lefts, rights = table[:, pl.ds(0, 1)], table[:, pl.ds(1, 1)]
        at_yc, order = moved(lefts)
        if to is ftab:
            lefts = at_yc * z_n + order
            at_yc, order = moved(rights)
            rights = at_yc * z_n + order
        else:
            lefts = order * yc_n + at_yc
        to[:, pl.ds(0, 1), span_o] = jnp.where(keep, lefts, grid_n)
        to[:, pl.ds(1, 1), span_o] = rights
    rows[0, lay] = jnp.concatenate([pad_row(sf_ref[...]), pad_row(sl_ref[...])], axis=1)
    first[grid_n] = jnp.zeros((width, width), BF)
    left[grid_n] = jnp.zeros((width, width), BF)
    load_x.wait()
    gathered[0][...] = x_ref[:, my_rows, :]
    pl.semaphore_wait(barrier, grid_n - 1 + 3 * yc_n)

    def hop(up, k, s):
        if k == 1:
            src = 0
        else:
            src = slot_order(-(k - 1) if up else k - 1, z_n)
        dst = slot_order(-k if up else k, z_n)
        span = pl.ds(s * sub, sub)
        which = 0 if up else 1
        return pltpu.make_async_remote_copy(
            src_ref=gathered[src].at[span],
            dst_ref=gathered[dst].at[span],
            send_sem=ring_send.at[which, k - 1, s],
            recv_sem=ring_recv.at[which, k - 1, s],
            device_id=at_z(1 if up else -1),
            device_id_type=MESH,
        )

    def hops():
        return [(up, s) for s in range(SUBS) for up in (True, False)]

    def tab_copy(step):
        return pltpu.make_async_remote_copy(
            src_ref=tabs.at[lay],
            dst_ref=tabs.at[lay],
            send_sem=tab_send.at[step - 1],
            recv_sem=tab_recv.at[step - 1],
            device_id=(me, lays[step]),
            device_id_type=MESH,
        )

    def row_copy(step):
        return pltpu.make_async_remote_copy(
            src_ref=rows.at[0, lay],
            dst_ref=rows.at[0, lay],
            send_sem=row_send.at[step - 1],
            recv_sem=row_recv.at[step - 1],
            device_id=(me, lays[step]),
            device_id_type=MESH,
        )

    def rows_copy(step):
        return pltpu.make_async_remote_copy(
            src_ref=rows.at[0],
            dst_ref=rows.at[slot_order(-step, z_n)],
            send_sem=row_send.at[2 + step % z_n],
            recv_sem=row_recv.at[2 + step % z_n],
            device_id=at_z(step),
            device_id_type=MESH,
        )

    for step in range(1, 4):
        row_copy(step).start()
    for up, s in hops():
        hop(up, 1, s).start()
    for step in range(1, 4):
        tab_copy(step).start()
    for step in range(1, 4):
        row_copy(step).wait_recv()
    near = [step for k in range(1, reach + 1) for step in (k, -k)]
    for step in near:
        rows_copy(step).start()
    for step in near:
        rows_copy(step).wait_recv()
    for step in range(1, 4):
        tab_copy(step).wait_recv()
    moves = [
        pltpu.make_async_copy(rows, srows, loc_sem.at[0]),
        pltpu.make_async_copy(tabs, stab, loc_sem.at[1]),
        pltpu.make_async_copy(ftab, sftab, loc_sem.at[2]),
    ]
    for move in moves:
        move.start()
    for move in moves:
        move.wait()

    def group(k):
        if k == 0:
            return 0, 1
        return 2 * k - 1, 2

    def plane_copy(src, dst, which, low, count, d, to):
        return pltpu.make_async_remote_copy(
            src_ref=src,
            dst_ref=dst.at[pl.ds(yc * z_n + low, count), my_rows],
            send_sem=send_sem.at[which],
            recv_sem=recv_sem.at[which],
            device_id=(d, to),
            device_id_type=MESH,
        )

    def plane_send(src, dst, which, k):
        low, count = group(k)

        def one(i, d, to):
            plane_copy(src.at[i, pl.ds(low, count)], dst, which, low, count, d, to).start()

        each_mate(0, yc_n, one)
        dst[pl.ds(yc * z_n + low, count), my_rows] = src[0, pl.ds(low, count)]

    def left_direct(pieces):
        for r in pieces:
            slots = pl.ds(r * yc_n + yc, 1)

            def one(i, d, to):
                pltpu.make_async_remote_copy(
                    src_ref=lstage.at[i, pl.ds(r, 1)],
                    dst_ref=left.at[slots, my_rows],
                    send_sem=send_sem.at[1],
                    recv_sem=recv_sem.at[1],
                    device_id=(d, to),
                    device_id_type=MESH,
                ).start()

            each_mate(0, yc_n, one)
            left[slots, my_rows] = lstage[0, pl.ds(r, 1)]

    def left_across(piece, src_of):
        slot = piece * yc_n + yc

        def one(m, carry):
            pltpu.make_async_remote_copy(
                src_ref=src_of(m),
                dst_ref=mid.at[:, slot],
                send_sem=send_sem.at[3],
                recv_sem=recv_sem.at[3],
                device_id=(zs[0] + mate_yc(m), lay),
                device_id_type=MESH,
            ).start()
            return carry

        lax.fori_loop(1, yc_n, one, 0)
        mid[:, slot] = src_of(0)[...]

    def cross_copy(dx):
        return pltpu.make_async_remote_copy(
            src_ref=mid.at[dx],
            dst_ref=left.at[pl.ds(mid_low, mid_n), my_rows],
            send_sem=cross_send.at[dx - 1],
            recv_sem=cross_recv.at[dx - 1],
            device_id=(me, lays[dx]),
            device_id_type=MESH,
        )

    def first_picks(r, d, put):
        for dx in range(4):
            put(dx, gathered[r][srows[r, lays[dx], 0, d]])

    lane_q = lax.broadcasted_iota(jnp.int32, (quarter, width), 1) // quarter

    def swap(a, b, groups):
        w = groups * quarter
        low = (lane_q // groups) % 2 == 0
        return (
            jnp.where(low, a, pltpu.roll(b, w, 1)),
            jnp.where(low, pltpu.roll(a, width - w, 1), b),
        )

    backs = [lax.rem(q - lay + 4, 4) for q in range(4)]

    def left_picks(r, d, put):
        p0, p1, p2, p3 = [
            gathered[r][srows[r, j, 0, HALF + d]].astype(F32) for j in range(4)
        ]
        t0, t2 = swap(p0, p2, 2)
        t1, t3 = swap(p1, p3, 2)
        q0, q1 = swap(t0, t1, 1)
        q2, q3 = swap(t2, t3, 1)
        for q, piece in enumerate((q0, q1, q2, q3)):
            put(backs[q], piece.astype(BF))

    def fill_group(picks, dst, k):
        low, count = group(k)

        def one(m, carry):
            d = zs[0] + mate_yc(m)
            for r in range(low, low + count):

                def put(dx, value):
                    dst[m * 4 + dx, r] = value

                picks(r, d, put)
            return carry

        lax.fori_loop(0, yc_n, one, 0)

    whole_steps = list(range(1, half_z - reach))
    far_n = 2 * len(whole_steps) + 1
    far_low = 2 * reach + 1
    last_step = half_z - reach

    def far_parts():
        out = [(last_step, 0)]
        for e in whole_steps:
            out += [(e, 0), (e, 1)]
        return out

    def fill_far(picks, dst, seg):
        e, h = far_parts()[seg]
        for up in (True, False):
            r = slot_order(-reach if up else reach, z_n)
            which = 0 if up else 1
            span = h if e < last_step else which

            def one(m, carry):
                d = zs[(e if up else -e) % z_n] + mate_yc(m)

                def put(dx, value):
                    dst[which, e - 1, m * 4 + dx] = value

                picks(r, d, put)
                return carry

            lax.fori_loop(span * (yc_n // 2), (span + 1) * (yc_n // 2), one, 0)

    def far_copy(src, dst, kind, up, seg):
        e, h = far_parts()[seg]
        which = 0 if up else 1
        span = pl.ds((h if e < last_step else which) * half_plane, half_plane)
        slot = slot_order(-(reach + e) if up else reach + e, z_n) - far_low
        return pltpu.make_async_remote_copy(
            src_ref=src.at[which, e - 1, span],
            dst_ref=dst.at[slot, span],
            send_sem=far_send.at[kind, which, seg],
            recv_sem=far_recv.at[kind, which, seg],
            device_id=at_z(e if up else -e),
            device_id_type=MESH,
        )

    def far_plane_send(src, dst, which, low, count, m_low, m_high):
        def one(i, d, to):
            piece = src.at[pl.ds(low, count), i]
            plane_copy(piece, dst, which, far_low + low, count, d, to).start()

        each_mate(m_low, m_high, one)
        if m_low == 0:
            dst[pl.ds(yc * z_n + far_low + low, count), my_rows] = src[pl.ds(low, count), 0]

    def arrive(k):
        for up, s in hops():
            hop(up, k, s).wait_recv()
            if k < reach:
                hop(up, k + 1, s).start()

    both = (True, False)
    parts = range(len(far_parts()))
    for k in range(0, reach + 1):
        if k > 0:
            arrive(k)
        if k == reach:
            for seg in parts:
                fill_far(first_picks, far_out, seg)
                for up in both:
                    far_copy(far_out, far_in, 0, up, seg).start()
        fill_group(first_picks, stage, k)
        plane_send(stage, first, 0, k)
        fill_group(left_picks, lstage, k)
        if k < reach:
            low, count = group(k)
            left_direct(range(low, low + count))
    for seg in parts:
        fill_far(left_picks, lfar_out, seg)
    for seg in parts:
        for up in both:
            far_copy(far_out, far_in, 0, up, seg).wait_recv()
        if seg == 0:
            far_plane_send(far_in, first, 0, far_n - 1, 1, 0, yc_n)
        else:
            e, h = far_parts()[seg]
            half = yc_n // 2
            far_plane_send(far_in, first, 0, 2 * e - 2, 2, h * half, (h + 1) * half)
    for seg in parts:
        for up in both:
            far_copy(lfar_out, lfar_in, 1, up, seg).start()
    near_pieces = 2 * reach - 1 + DIRECT
    mid_low = near_pieces * yc_n
    mid_n = grid_n - mid_low
    left_direct(range(2 * reach - 1, near_pieces))
    for r in range(2 - DIRECT):
        left_across(r, lambda m, r=r: lstage.at[pl.ds(m * 4, 4), near_pieces + r])

    def wait_all(src, sem):
        whole = src.at[pl.ds(1, src.shape[0] - 1)]
        pltpu.make_async_copy(whole, whole, sem).wait()

    def wait_plane(dst, sem):
        whole = dst.at[pl.ds(0, (plane_n - 1) * z_n // 4)]
        pltpu.make_async_copy(whole, whole, sem).wait()

    wait_plane(first, recv_sem.at[0])

    right_lay, left_lay, far_lay = lays[1], lays[3], lays[2]

    def rows_of(q, h):
        return pl.ds(pl.multiple_of(q * quarter + h * ROWS, ROWS), ROWS)

    def reduce_rows(phase, together, product, src, got, comb, midway, finish):
        def copy(kind, c):
            span = pl.ds(c * per, per)
            if kind == 0:
                ref, to = src.at[span, rows_of(far_lay, 0)], right_lay
            elif kind == 1:
                ref, to = src.at[span, rows_of(far_lay, 1)], left_lay
            elif kind == 2:
                ref, to = src.at[span, rows_of(right_lay, 1)], right_lay
            elif kind == 3:
                ref, to = src.at[span, rows_of(left_lay, 0)], left_lay
            elif kind == 4:
                ref, to = comb.at[0, span], right_lay
            else:
                ref, to = comb.at[1, span], left_lay
            return pltpu.make_async_remote_copy(
                src_ref=ref,
                dst_ref=got.at[kind, span],
                send_sem=rs_send.at[phase, kind, c],
                recv_sem=rs_recv.at[phase, kind, c],
                device_id=(me, to),
                device_id_type=MESH,
            )

        def relay(c):
            span = pl.ds(c * per, per)
            for kind, q in ((0, right_lay), (1, left_lay)):
                copy(kind, c).wait_recv()
                own = src[span, rows_of(q, kind)].astype(F32)
                comb[kind, span] = (own + got[kind, span].astype(F32)).astype(BF)
                copy(4 + kind, c).start()

        def chunk(c, carry):
            def some(i, inner):
                for n in range(together):
                    product(c * per + i * together + n)
                return inner

            lax.fori_loop(0, per // together, some, 0)
            for kind in range(4):
                copy(kind, c).start()

            @pl.when(c >= LAG)
            def _():
                relay(c - LAG)

            @pl.when(c == CHUNKS // 2 - 1)
            def _():
                midway()

            return carry

        lax.fori_loop(0, CHUNKS, chunk, 0)
        def close(c, carry):
            span = pl.ds(c * per, per)
            for h, direct, joined in ((0, 3, 4), (1, 2, 5)):
                copy(direct, c).wait_recv()
                copy(joined, c).wait_recv()
                total = (
                    src[span, rows_of(lay, h)].astype(F32)
                    + got[direct, span].astype(F32)
                    + got[joined, span].astype(F32)
                )
                finish(span, h, total)
            return carry

        for c in range(CHUNKS - LAG, CHUNKS):
            if c == CHUNKS - 1:
                lax.fori_loop(0, CHUNKS // 2, close, 0)
            relay(c)
        lax.fori_loop(CHUNKS // 2, CHUNKS, close, 0)

        def drain(c, carry):
            for kind in range(6):
                copy(kind, c).wait_send()
            return carry

        return drain

    def product_first(o):
        acc = jnp.zeros((width, width), F32)
        for t in range(0, terms, 2):
            a = jnp.concatenate([first[sftab[u, 0, o]] for u in (t, t + 1)], axis=1)
            b = jnp.concatenate([first[sftab[u, 1, o]] for u in (t, t + 1)], axis=0)
            acc = acc + jnp.dot(a, b, preferred_element_type=F32)
        part[o] = acc.astype(BF)

    def finish_first(span, h, total):
        sq_ref[span, pl.ds(h * ROWS, ROWS)] = total.astype(BF)

    def send_late():
        for seg in parts:
            for up in both:
                far_copy(lfar_out, lfar_in, 1, up, seg).wait_recv()
        for f in range(far_n):
            left_across(2 - DIRECT + f, lambda m, f=f: lfar_in.at[f, pl.ds(m * 4, 4)])

    def wait_mid(sem):
        whole = mid.at[:, pl.ds(0, mid_n // yc_n * (yc_n - 1))]
        pltpu.make_async_copy(whole, whole, sem).wait()

    def send_cross():
        wait_mid(recv_sem.at[3])
        for dx in (1, 2, 3):
            cross_copy(dx).start()

    drain_first = reduce_rows(
        0, 4, product_first, part, rs1, comb1, send_late, finish_first
    )

    def send_right(i, d):
        rstage[i] = sq_ref[ssr[0, d]]
        pltpu.make_async_remote_copy(
            src_ref=rstage.at[i],
            dst_ref=right.at[me],
            send_sem=send_sem.at[2],
            recv_sem=recv_sem.at[2],
            device_id=(d, lay),
            device_id_type=MESH,
        ).start()

    each_peer(send_right)
    right[me] = sq_ref[ssr[0, me]]
    send_cross()
    left[pl.ds(mid_low, mid_n), my_rows] = mid[0]

    def wait_direct(sem):
        whole = lstage.at[pl.ds(1, plane_n - 1), pl.ds(0, near_pieces)]
        pltpu.make_async_copy(whole, whole, sem).wait()

    wait_direct(recv_sem.at[1])
    for dx in (1, 2, 3):
        cross_copy(dx).wait_recv()
    wait_all(rstage, recv_sem.at[2])

    lane = lax.broadcasted_iota(jnp.int32, (width, width), 1) // quarter

    def product_second(o):
        acc = jnp.zeros((width, width), F32)
        for t in range(0, terms, 2):
            a_parts, b_parts = [], []
            for u in (t, t + 1):
                lefts = [left[stab[j, u, 0, o]] for j in range(4)]
                low = jnp.where(lane == 0, lefts[0], lefts[1])
                high = jnp.where(lane == 2, lefts[2], lefts[3])
                a_parts.append(jnp.where(lane < 2, low, high))
                b_parts += [right[stab[j, u, 1, o]] for j in range(4)]
            a = jnp.concatenate(a_parts, axis=1)
            b = jnp.concatenate(b_parts, axis=0)
            acc = acc + jnp.dot(a, b, preferred_element_type=F32)
        part2[o] = acc.astype(BF)

    def finish_second(span, h, total):
        own = x_ref[span, rows_of(lay, h)].astype(F32)
        out_ref[span, pl.ds(h * ROWS, ROWS)] = (1.5 * own - 0.5 * total).astype(BF)

    drain_second = reduce_rows(
        1, 8, product_second, part2, rs2, comb2, lambda: None, finish_second
    )

    lax.fori_loop(0, CHUNKS, drain_first, 0)
    lax.fori_loop(0, CHUNKS, drain_second, 0)
    for k in range(1, reach + 1):
        for up, s in hops():
            hop(up, k, s).wait_send()
    for step in range(1, 4):
        tab_copy(step).wait_send()
        row_copy(step).wait_send()
    for step in near:
        rows_copy(step).wait_send()
    for seg in parts:
        for up in both:
            far_copy(far_out, far_in, 0, up, seg).wait_send()
            far_copy(lfar_out, lfar_in, 1, up, seg).wait_send()
    wait_plane(first, send_sem.at[0])
    wait_direct(send_sem.at[1])
    wait_mid(send_sem.at[3])
    for dx in (1, 2, 3):
        cross_copy(dx).wait_send()
    wait_all(rstage, send_sem.at[2])


def local(
    y_n,
    x_blocks,
    send_first,
    send_left,
    send_right,
    terms_first,
    terms_second,
    live_first,
    live_second,
):
    grid_n = lax.axis_size("grid")
    blocks, width = x_blocks.shape[0], x_blocks.shape[1]
    count = terms_first.shape[2]
    quarter = width // 4
    yc_n = 2 * y_n
    z_n = grid_n // yc_n

    reach = z_n // 4
    steps = z_n // 2 - reach
    near_n = 2 * reach + 1

    def by_term(table):
        return table.reshape(blocks, count, 2).transpose(1, 2, 0)

    small = (
        send_first.reshape(1, grid_n),
        send_left.reshape(1, grid_n),
        send_right.reshape(1, grid_n),
        by_term(terms_first),
        by_term(terms_second),
        live_first.reshape(1, blocks),
        live_second.reshape(1, blocks),
    )
    share = jax.ShapeDtypeStruct((blocks, quarter, width), BF)
    vmem = pl.BlockSpec(memory_space=pltpu.VMEM)
    dma = pltpu.SemaphoreType.DMA
    return pl.pallas_call(
        functools.partial(kernel, grid_n, y_n, blocks, count),
        out_shape=(share, share),
        in_specs=[pl.BlockSpec(memory_space=pl.ANY)] * 8,
        out_specs=(vmem, vmem),
        scratch_shapes=[
            pltpu.VMEM((1, grid_n), jnp.int32),
            pltpu.VMEM((1, grid_n), jnp.int32),
            pltpu.SMEM((1, grid_n), jnp.int32),
            pltpu.VMEM((count, 2, blocks), jnp.int32),
            pltpu.VMEM((count, 2, blocks), jnp.int32),
            pltpu.VMEM((1, blocks), jnp.int32),
            pltpu.VMEM((1, blocks), jnp.int32),
            pltpu.VMEM((blocks, width, width), BF),
            *[pltpu.VMEM((blocks, quarter, width), BF)] * near_n,
            pltpu.VMEM((yc_n * 4, near_n, quarter, width), BF),
            pltpu.VMEM((yc_n * 4, near_n, quarter, width), BF),
            pltpu.VMEM((2, steps, yc_n * 4, quarter, width), BF),
            pltpu.VMEM((z_n - near_n, yc_n * 4, quarter, width), BF),
            pltpu.VMEM((2, steps, yc_n * 4, quarter, width), BF),
            pltpu.VMEM((z_n - near_n, yc_n * 4, quarter, width), BF),
            pltpu.VMEM((4, grid_n - (2 * reach - 1 + DIRECT) * yc_n, quarter, width), BF),
            pltpu.VMEM((grid_n, quarter, width), BF),
            pltpu.VMEM((grid_n + 1, width, width), BF),
            pltpu.VMEM((grid_n + 1, width, width), BF),
            pltpu.VMEM((grid_n, quarter, width), BF),
            pltpu.VMEM((blocks, width, width), BF),
            pltpu.VMEM((blocks, width, width), BF),
            pltpu.VMEM((6, blocks, ROWS, width), BF),
            pltpu.VMEM((6, blocks, ROWS, width), BF),
            pltpu.VMEM((2, blocks, ROWS, width), BF),
            pltpu.VMEM((2, blocks, ROWS, width), BF),
            pltpu.VMEM((count, 2, 128), jnp.int32),
            pltpu.SMEM((count, 2, 128), jnp.int32),
            pltpu.VMEM((4, count, 2, 128), jnp.int32),
            pltpu.SMEM((4, count, 2, 128), jnp.int32),
            pltpu.VMEM((near_n, 4, 1, 128), jnp.int32),
            pltpu.SMEM((near_n, 4, 1, 128), jnp.int32),
            dma((4,)),
            dma((4,)),
            dma((2, reach, SUBS)),
            dma((2, reach, SUBS)),
            dma((2, 2, 2 * steps - 1)),
            dma((2, 2, 2 * steps - 1)),
            dma((3,)),
            dma((3,)),
            dma((3,)),
            dma((3,)),
            dma((2 + z_n,)),
            dma((2 + z_n,)),
            dma((10,)),
            dma((2, 6, CHUNKS)),
            dma((2, 6, CHUNKS)),
        ],
        compiler_params=pltpu.CompilerParams(
            collective_id=0, has_side_effects=True, vmem_limit_bytes=60 * 1024 * 1024
        ),
    )(x_blocks, *small)


def solution(mesh, y_n=4):
    return jax.shard_map(
        functools.partial(local, y_n),
        mesh=mesh,
        in_specs=(
            P("grid", None, None),
            P("grid", "layer", None, None),
            P("grid", "layer", None, None),
            P("grid", None, None),
            P("grid", "layer", None, None),
            P("grid", "layer", None, None),
            P("grid", "layer"),
            P("grid", "layer"),
        ),
        out_specs=(P("grid", "layer", None), P("grid", "layer", None)),
        check_vma=False,
    )
```

```python
import functools

import jax
import jax.numpy as jnp
from jax import lax
from jax.experimental import pallas as pl
from jax.experimental.pallas import tpu as pltpu
from jax.sharding import PartitionSpec as P

MESH = pl.DeviceIdType.MESH
BF = jnp.bfloat16
F32 = jnp.float32
HALF = 64
CHUNKS = 8
LAG = 2
DIRECT = 0
FAR_FIRST = (4, 3, 5, 2, 6, 1, 7)
ROWS = 16
SUBS = 2


def slot_order(k, n):
    k = k % n
    return 0 if k == 0 else (2 * k - 1 if 2 * k <= n else 2 * (n - k))


def kernel(grid_n, y_n, blocks, terms, x_hbm, *refs):
    near_n = 2 * (grid_n // (2 * y_n) // 4) + 1
    small, outs, refs = refs[:7], refs[7:9], refs[9:]
    held, x_ref, gathered, rest = refs[:7], refs[7], refs[8 : 8 + near_n], refs[8 + near_n :]
    run(grid_n, y_n, blocks, terms, x_hbm, small, *held, *outs, x_ref, gathered, *rest)


def run(
    grid_n,
    y_n,
    blocks,
    terms,
    x_hbm,
    small,
    sf_ref,
    sl_ref,
    ssr,
    tf_ref,
    ts_ref,
    lf_ref,
    ls_ref,
    sq_ref,
    out_ref,
    x_ref,
    gathered,
    stage,
    lstage,
    far_out,
    far_in,
    lfar_out,
    lfar_in,
    mid,
    rstage,
    first,
    left,
    right,
    part,
    part2,
    rs1,
    rs2,
    comb1,
    comb2,
    ftab,
    sftab,
    tabs,
    stab,
    rows,
    srows,
    send_sem,
    recv_sem,
    ring_send,
    ring_recv,
    far_send,
    far_recv,
    cross_send,
    cross_recv,
    tab_send,
    tab_recv,
    row_send,
    row_recv,
    loc_sem,
    rs_send,
    rs_recv,
):
    me = lax.axis_index("grid")
    lay = lax.axis_index("layer")
    load_x = pltpu.make_async_copy(x_hbm, x_ref, loc_sem.at[0])
    held = (sf_ref, sl_ref, ssr, tf_ref, ts_ref, lf_ref, ls_ref)
    loads = [
        pltpu.make_async_copy(src, dst, loc_sem.at[3 + n])
        for n, (src, dst) in enumerate(zip(small, held))
    ]
    for load in (*loads, load_x):
        load.start()
    width = x_ref.shape[1]
    quarter = width // 4
    z_n = grid_n // (2 * y_n)
    yc_n = 2 * y_n
    z, y, core = me // yc_n, (me // 2) % y_n, me % 2
    yc = y * 2 + core
    per = blocks // CHUNKS
    sub = blocks // SUBS
    plane_n = yc_n * 4
    half_z = z_n // 2
    reach = half_z // 2
    half_plane = plane_n // 2
    zs = [lax.rem(z + dz, z_n) * yc_n for dz in range(z_n)]
    lays = [lax.rem(lay + dx, 4) for dx in range(4)]

    def mate_yc(m):
        return lax.rem(y + lax.div(m, 2), y_n) * 2 + lax.rem(core + m, 2)

    def at_z(dz):
        return (zs[dz % z_n] + yc, lay)

    def each_peer(act):
        def one(m, carry):
            other = mate_yc(m)
            for dz in FAR_FIRST:
                if 0 < dz < z_n:
                    act(m * z_n + dz, zs[dz] + other)

            @pl.when(m > 0)
            def _():
                act(m * z_n, zs[0] + other)

            return carry

        lax.fori_loop(0, yc_n, one, 0)

    def each_mate(low, high, act):
        def one(m, carry):
            d = zs[0] + mate_yc(m)
            for dx in range(1, 4):
                act(m * 4 + dx, d, lays[dx])

            @pl.when(m > 0)
            def _():
                act(m * 4, d, lay)

            return carry

        lax.fori_loop(low, high, one, 0)

    my_rows = pl.ds(pl.multiple_of(lay * quarter, quarter), quarter)

    barrier = pltpu.get_barrier_semaphore()

    def greet(d, to):
        pl.semaphore_signal(barrier, inc=1, device_id=(d, to), device_id_type=MESH)

    each_peer(lambda i, d: greet(d, lay))

    def greet_layers(m, carry):
        d = zs[0] + mate_yc(m)
        for dx in range(1, 4):
            greet(d, lays[dx])
        return carry

    lax.fori_loop(0, yc_n, greet_layers, 0)
    for load in loads:
        load.wait()

    def moved(slots):
        away = lax.rem(lax.div(slots, yc_n) - z + z_n, z_n)
        order = jnp.where(2 * away <= z_n, 2 * away - 1, 2 * (z_n - away))
        order = jnp.where(away == 0, 0, order)
        return lax.rem(slots, yc_n), order

    def pad_row(values):
        return jnp.pad(values, ((0, 0), (0, HALF - values.shape[1])))

    term = lax.broadcasted_iota(jnp.int32, (terms, 1, blocks), 0)
    span_o = pl.ds(0, blocks)
    for table, live, to in ((tf_ref, lf_ref, ftab), (ts_ref, ls_ref, tabs.at[lay])):
        keep = term < live[...].reshape(1, 1, blocks)
        to[...] = jnp.zeros(to.shape, jnp.int32)
        lefts, rights = table[:, pl.ds(0, 1)], table[:, pl.ds(1, 1)]
        at_yc, order = moved(lefts)
        if to is ftab:
            lefts = at_yc * z_n + order
            at_yc, order = moved(rights)
            rights = at_yc * z_n + order
        else:
            lefts = order * yc_n + at_yc
        to[:, pl.ds(0, 1), span_o] = jnp.where(keep, lefts, grid_n)
        to[:, pl.ds(1, 1), span_o] = rights
    rows[0, lay] = jnp.concatenate([pad_row(sf_ref[...]), pad_row(sl_ref[...])], axis=1)
    first[grid_n] = jnp.zeros((width, width), BF)
    left[grid_n] = jnp.zeros((width, width), BF)
    load_x.wait()
    gathered[0][...] = x_ref[:, my_rows, :]
    pl.semaphore_wait(barrier, grid_n - 1 + 3 * yc_n)

    def hop(up, k, s):
        if k == 1:
            src = 0
        else:
            src = slot_order(-(k - 1) if up else k - 1, z_n)
        dst = slot_order(-k if up else k, z_n)
        span = pl.ds(s * sub, sub)
        which = 0 if up else 1
        return pltpu.make_async_remote_copy(
            src_ref=gathered[src].at[span],
            dst_ref=gathered[dst].at[span],
            send_sem=ring_send.at[which, k - 1, s],
            recv_sem=ring_recv.at[which, k - 1, s],
            device_id=at_z(1 if up else -1),
            device_id_type=MESH,
        )

    def hops():
        return [(up, s) for s in range(SUBS) for up in (True, False)]

    def tab_copy(step):
        return pltpu.make_async_remote_copy(
            src_ref=tabs.at[lay],
            dst_ref=tabs.at[lay],
            send_sem=tab_send.at[step - 1],
            recv_sem=tab_recv.at[step - 1],
            device_id=(me, lays[step]),
            device_id_type=MESH,
        )

    def row_copy(step):
        return pltpu.make_async_remote_copy(
            src_ref=rows.at[0, lay],
            dst_ref=rows.at[0, lay],
            send_sem=row_send.at[step - 1],
            recv_sem=row_recv.at[step - 1],
            device_id=(me, lays[step]),
            device_id_type=MESH,
        )

    def rows_copy(step):
        return pltpu.make_async_remote_copy(
            src_ref=rows.at[0],
            dst_ref=rows.at[slot_order(-step, z_n)],
            send_sem=row_send.at[2 + step % z_n],
            recv_sem=row_recv.at[2 + step % z_n],
            device_id=at_z(step),
            device_id_type=MESH,
        )

    for step in range(1, 4):
        row_copy(step).start()
    for up, s in hops():
        hop(up, 1, s).start()
    for step in range(1, 4):
        tab_copy(step).start()
    for step in range(1, 4):
        row_copy(step).wait_recv()
    near = [step for k in range(1, reach + 1) for step in (k, -k)]
    for step in near:
        rows_copy(step).start()
    for step in near:
        rows_copy(step).wait_recv()
    for step in range(1, 4):
        tab_copy(step).wait_recv()
    moves = [
        pltpu.make_async_copy(rows, srows, loc_sem.at[0]),
        pltpu.make_async_copy(tabs, stab, loc_sem.at[1]),
        pltpu.make_async_copy(ftab, sftab, loc_sem.at[2]),
    ]
    for move in moves:
        move.start()
    for move in moves:
        move.wait()

    def group(k):
        if k == 0:
            return 0, 1
        return 2 * k - 1, 2

    def plane_copy(src, dst, which, low, count, d, to):
        return pltpu.make_async_remote_copy(
            src_ref=src,
            dst_ref=dst.at[pl.ds(yc * z_n + low, count), my_rows],
            send_sem=send_sem.at[which],
            recv_sem=recv_sem.at[which],
            device_id=(d, to),
            device_id_type=MESH,
        )

    def plane_send(src, dst, which, k):
        low, count = group(k)

        def one(i, d, to):
            plane_copy(src.at[i, pl.ds(low, count)], dst, which, low, count, d, to).start()

        each_mate(0, yc_n, one)
        dst[pl.ds(yc * z_n + low, count), my_rows] = src[0, pl.ds(low, count)]

    def left_direct(pieces):
        for r in pieces:
            slots = pl.ds(r * yc_n + yc, 1)

            def one(i, d, to):
                pltpu.make_async_remote_copy(
                    src_ref=lstage.at[i, pl.ds(r, 1)],
                    dst_ref=left.at[slots, my_rows],
                    send_sem=send_sem.at[1],
                    recv_sem=recv_sem.at[1],
                    device_id=(d, to),
                    device_id_type=MESH,
                ).start()

            each_mate(0, yc_n, one)
            left[slots, my_rows] = lstage[0, pl.ds(r, 1)]

    def left_across(piece, which, src_of):
        slot = piece * yc_n + yc

        def one(m, carry):
            pltpu.make_async_remote_copy(
                src_ref=src_of(m),
                dst_ref=mid.at[:, slot],
                send_sem=send_sem.at[which],
                recv_sem=recv_sem.at[which],
                device_id=(zs[0] + mate_yc(m), lay),
                device_id_type=MESH,
            ).start()
            return carry

        lax.fori_loop(1, yc_n, one, 0)
        mid[:, slot] = src_of(0)[...]

    def cross_copy(dx, part_of):
        early = (2 - DIRECT) * yc_n
        low, count = ((0, early), (early, mid_n - early))[part_of]
        return pltpu.make_async_remote_copy(
            src_ref=mid.at[dx, pl.ds(low, count)],
            dst_ref=left.at[pl.ds(mid_low + low, count), my_rows],
            send_sem=cross_send.at[part_of, dx - 1],
            recv_sem=cross_recv.at[part_of, dx - 1],
            device_id=(me, lays[dx]),
            device_id_type=MESH,
        )

    def first_picks(r, d, put):
        for dx in range(4):
            put(dx, gathered[r][srows[r, lays[dx], 0, d]])

    lane_q = lax.broadcasted_iota(jnp.int32, (quarter, width), 1) // quarter

    def swap(a, b, groups):
        w = groups * quarter
        low = (lane_q // groups) % 2 == 0
        return (
            jnp.where(low, a, pltpu.roll(b, w, 1)),
            jnp.where(low, pltpu.roll(a, width - w, 1), b),
        )

    backs = [lax.rem(q - lay + 4, 4) for q in range(4)]

    def left_picks(r, d, put):
        p0, p1, p2, p3 = [
            gathered[r][srows[r, j, 0, HALF + d]].astype(F32) for j in range(4)
        ]
        t0, t2 = swap(p0, p2, 2)
        t1, t3 = swap(p1, p3, 2)
        q0, q1 = swap(t0, t1, 1)
        q2, q3 = swap(t2, t3, 1)
        for q, piece in enumerate((q0, q1, q2, q3)):
            put(backs[q], piece.astype(BF))

    def fill_group(picks, dst, k):
        low, count = group(k)

        def one(m, carry):
            d = zs[0] + mate_yc(m)
            for r in range(low, low + count):

                def put(dx, value):
                    dst[m * 4 + dx, r] = value

                picks(r, d, put)
            return carry

        lax.fori_loop(0, yc_n, one, 0)

    whole_steps = list(range(1, half_z - reach))
    far_n = 2 * len(whole_steps) + 1
    far_low = 2 * reach + 1
    last_step = half_z - reach

    def far_parts():
        out = [(last_step, 0)]
        for e in whole_steps:
            out += [(e, 0), (e, 1)]
        return out

    def fill_far(picks, dst, seg):
        e, h = far_parts()[seg]
        for up in (True, False):
            r = slot_order(-reach if up else reach, z_n)
            which = 0 if up else 1
            span = h if e < last_step else which

            def one(m, carry):
                d = zs[(e if up else -e) % z_n] + mate_yc(m)

                def put(dx, value):
                    dst[which, e - 1, m * 4 + dx] = value

                picks(r, d, put)
                return carry

            lax.fori_loop(span * (yc_n // 2), (span + 1) * (yc_n // 2), one, 0)

    def far_copy(src, dst, kind, up, seg):
        e, h = far_parts()[seg]
        which = 0 if up else 1
        span = pl.ds((h if e < last_step else which) * half_plane, half_plane)
        slot = slot_order(-(reach + e) if up else reach + e, z_n) - far_low
        return pltpu.make_async_remote_copy(
            src_ref=src.at[which, e - 1, span],
            dst_ref=dst.at[slot, span],
            send_sem=far_send.at[kind, which, seg],
            recv_sem=far_recv.at[kind, which, seg],
            device_id=at_z(e if up else -e),
            device_id_type=MESH,
        )

    def far_plane_send(src, dst, which, low, count, m_low, m_high):
        def one(i, d, to):
            piece = src.at[pl.ds(low, count), i]
            plane_copy(piece, dst, which, far_low + low, count, d, to).start()

        each_mate(m_low, m_high, one)
        if m_low == 0:
            dst[pl.ds(yc * z_n + far_low + low, count), my_rows] = src[pl.ds(low, count), 0]

    def arrive(k):
        for up, s in hops():
            hop(up, k, s).wait_recv()
            if k < reach:
                hop(up, k + 1, s).start()

    both = (True, False)
    parts = range(len(far_parts()))
    for k in range(0, reach + 1):
        if k > 0:
            arrive(k)
        if k == reach:
            for seg in parts:
                fill_far(first_picks, far_out, seg)
                for up in both:
                    far_copy(far_out, far_in, 0, up, seg).start()
        fill_group(first_picks, stage, k)
        plane_send(stage, first, 0, k)
        fill_group(left_picks, lstage, k)
        if k < reach:
            low, count = group(k)
            left_direct(range(low, low + count))
    for seg in parts:
        fill_far(left_picks, lfar_out, seg)
    for seg in parts:
        for up in both:
            far_copy(far_out, far_in, 0, up, seg).wait_recv()
        if seg == 0:
            far_plane_send(far_in, first, 0, far_n - 1, 1, 0, yc_n)
        else:
            e, h = far_parts()[seg]
            half = yc_n // 2
            far_plane_send(far_in, first, 0, 2 * e - 2, 2, h * half, (h + 1) * half)
    for seg in parts:
        for up in both:
            far_copy(lfar_out, lfar_in, 1, up, seg).start()
    near_pieces = 2 * reach - 1 + DIRECT
    mid_low = near_pieces * yc_n
    mid_n = grid_n - mid_low
    left_direct(range(2 * reach - 1, near_pieces))
    for r in range(2 - DIRECT):
        left_across(r, 3, lambda m, r=r: lstage.at[pl.ds(m * 4, 4), near_pieces + r])

    def wait_all(src, sem):
        whole = src.at[pl.ds(1, src.shape[0] - 1)]
        pltpu.make_async_copy(whole, whole, sem).wait()

    def wait_plane(dst, sem):
        whole = dst.at[pl.ds(0, (plane_n - 1) * z_n // 4)]
        pltpu.make_async_copy(whole, whole, sem).wait()

    wait_plane(first, recv_sem.at[0])

    right_lay, left_lay, far_lay = lays[1], lays[3], lays[2]

    def rows_of(q, h):
        return pl.ds(pl.multiple_of(q * quarter + h * ROWS, ROWS), ROWS)

    def reduce_rows(phase, together, product, src, got, comb, midway, between, finish):
        def copy(kind, c):
            span = pl.ds(c * per, per)
            if kind == 0:
                ref, to = src.at[span, rows_of(far_lay, 0)], right_lay
            elif kind == 1:
                ref, to = src.at[span, rows_of(far_lay, 1)], left_lay
            elif kind == 2:
                ref, to = src.at[span, rows_of(right_lay, 1)], right_lay
            elif kind == 3:
                ref, to = src.at[span, rows_of(left_lay, 0)], left_lay
            elif kind == 4:
                ref, to = comb.at[0, span], right_lay
            else:
                ref, to = comb.at[1, span], left_lay
            return pltpu.make_async_remote_copy(
                src_ref=ref,
                dst_ref=got.at[kind, span],
                send_sem=rs_send.at[phase, kind, c],
                recv_sem=rs_recv.at[phase, kind, c],
                device_id=(me, to),
                device_id_type=MESH,
            )

        def relay(c):
            span = pl.ds(c * per, per)
            for kind, q in ((0, right_lay), (1, left_lay)):
                copy(kind, c).wait_recv()
                own = src[span, rows_of(q, kind)].astype(F32)
                comb[kind, span] = (own + got[kind, span].astype(F32)).astype(BF)
                copy(4 + kind, c).start()

        def chunk(c, carry):
            def some(i, inner):
                for n in range(together):
                    product(c * per + i * together + n)
                return inner

            lax.fori_loop(0, per // together, some, 0)
            for kind in range(4):
                copy(kind, c).start()

            @pl.when(c >= LAG)
            def _():
                relay(c - LAG)

            @pl.when(c == 1)
            def _():
                midway()

            return carry

        lax.fori_loop(0, CHUNKS, chunk, 0)
        def close(c, carry):
            span = pl.ds(c * per, per)
            for h, direct, joined in ((0, 3, 4), (1, 2, 5)):
                copy(direct, c).wait_recv()
                copy(joined, c).wait_recv()
                total = (
                    src[span, rows_of(lay, h)].astype(F32)
                    + got[direct, span].astype(F32)
                    + got[joined, span].astype(F32)
                )
                finish(span, h, total)
            return carry

        for c in range(CHUNKS - LAG, CHUNKS):
            if c == CHUNKS - 1:
                lax.fori_loop(0, CHUNKS // 2, close, 0)
            relay(c)
        between()
        lax.fori_loop(CHUNKS // 2, CHUNKS, close, 0)

        def drain(c, carry):
            for kind in range(6):
                copy(kind, c).wait_send()
            return carry

        return drain

    def product_first(o):
        acc = jnp.zeros((width, width), F32)
        for t in range(0, terms, 2):
            a = jnp.concatenate([first[sftab[u, 0, o]] for u in (t, t + 1)], axis=1)
            b = jnp.concatenate([first[sftab[u, 1, o]] for u in (t, t + 1)], axis=0)
            acc = acc + jnp.dot(a, b, preferred_element_type=F32)
        part[o] = acc.astype(BF)

    def finish_first(span, h, total):
        sq_ref[span, pl.ds(h * ROWS, ROWS)] = total.astype(BF)

    def send_late():
        for seg in parts:
            for up in both:
                far_copy(lfar_out, lfar_in, 1, up, seg).wait_recv()
        for f in range(far_n):
            left_across(2 - DIRECT + f, 4, lambda m, f=f: lfar_in.at[f, pl.ds(m * 4, 4)])

    def wait_mid(part_of, sem):
        pieces = (2 - DIRECT, far_n)[part_of]
        whole = mid.at[:, pl.ds(0, pieces * (yc_n - 1))]
        pltpu.make_async_copy(whole, whole, sem).wait()

    def send_cross(part_of):
        wait_mid(part_of, recv_sem.at[3 + part_of])
        for dx in (1, 2, 3):
            cross_copy(dx, part_of).start()

    drain_first = reduce_rows(
        0, 4, product_first, part, rs1, comb1, send_late, lambda: send_cross(0), finish_first
    )

    def send_right(i, d):
        rstage[i] = sq_ref[ssr[0, d]]
        pltpu.make_async_remote_copy(
            src_ref=rstage.at[i],
            dst_ref=right.at[me],
            send_sem=send_sem.at[2],
            recv_sem=recv_sem.at[2],
            device_id=(d, lay),
            device_id_type=MESH,
        ).start()

    each_peer(send_right)
    right[me] = sq_ref[ssr[0, me]]
    send_cross(1)
    left[pl.ds(mid_low, mid_n), my_rows] = mid[0]

    def wait_direct(sem):
        whole = lstage.at[pl.ds(1, plane_n - 1), pl.ds(0, near_pieces)]
        pltpu.make_async_copy(whole, whole, sem).wait()

    wait_direct(recv_sem.at[1])
    for dx in (1, 2, 3):
        cross_copy(dx, 0).wait_recv()
        cross_copy(dx, 1).wait_recv()
    wait_all(rstage, recv_sem.at[2])

    lane = lax.broadcasted_iota(jnp.int32, (width, width), 1) // quarter

    def product_second(o):
        acc = jnp.zeros((width, width), F32)
        for t in range(0, terms, 2):
            a_parts, b_parts = [], []
            for u in (t, t + 1):
                lefts = [left[stab[j, u, 0, o]] for j in range(4)]
                low = jnp.where(lane == 0, lefts[0], lefts[1])
                high = jnp.where(lane == 2, lefts[2], lefts[3])
                a_parts.append(jnp.where(lane < 2, low, high))
                b_parts += [right[stab[j, u, 1, o]] for j in range(4)]
            a = jnp.concatenate(a_parts, axis=1)
            b = jnp.concatenate(b_parts, axis=0)
            acc = acc + jnp.dot(a, b, preferred_element_type=F32)
        part2[o] = acc.astype(BF)

    def finish_second(span, h, total):
        own = x_ref[span, rows_of(lay, h)].astype(F32)
        out_ref[span, pl.ds(h * ROWS, ROWS)] = (1.5 * own - 0.5 * total).astype(BF)

    drain_second = reduce_rows(
        1, 8, product_second, part2, rs2, comb2, lambda: None, lambda: None, finish_second
    )

    lax.fori_loop(0, CHUNKS, drain_first, 0)
    lax.fori_loop(0, CHUNKS, drain_second, 0)
    for k in range(1, reach + 1):
        for up, s in hops():
            hop(up, k, s).wait_send()
    for step in range(1, 4):
        tab_copy(step).wait_send()
        row_copy(step).wait_send()
    for step in near:
        rows_copy(step).wait_send()
    for seg in parts:
        for up in both:
            far_copy(far_out, far_in, 0, up, seg).wait_send()
            far_copy(lfar_out, lfar_in, 1, up, seg).wait_send()
    wait_plane(first, send_sem.at[0])
    wait_direct(send_sem.at[1])
    wait_mid(0, send_sem.at[3])
    wait_mid(1, send_sem.at[4])
    for dx in (1, 2, 3):
        cross_copy(dx, 0).wait_send()
        cross_copy(dx, 1).wait_send()
    wait_all(rstage, send_sem.at[2])


def local(
    y_n,
    x_blocks,
    send_first,
    send_left,
    send_right,
    terms_first,
    terms_second,
    live_first,
    live_second,
):
    grid_n = lax.axis_size("grid")
    blocks, width = x_blocks.shape[0], x_blocks.shape[1]
    count = terms_first.shape[2]
    quarter = width // 4
    yc_n = 2 * y_n
    z_n = grid_n // yc_n

    reach = z_n // 4
    steps = z_n // 2 - reach
    near_n = 2 * reach + 1

    def by_term(table):
        return table.reshape(blocks, count, 2).transpose(1, 2, 0)

    small = (
        send_first.reshape(1, grid_n),
        send_left.reshape(1, grid_n),
        send_right.reshape(1, grid_n),
        by_term(terms_first),
        by_term(terms_second),
        live_first.reshape(1, blocks),
        live_second.reshape(1, blocks),
    )
    share = jax.ShapeDtypeStruct((blocks, quarter, width), BF)
    vmem = pl.BlockSpec(memory_space=pltpu.VMEM)
    dma = pltpu.SemaphoreType.DMA
    return pl.pallas_call(
        functools.partial(kernel, grid_n, y_n, blocks, count),
        out_shape=(share, share),
        in_specs=[pl.BlockSpec(memory_space=pl.ANY)] * 8,
        out_specs=(vmem, vmem),
        scratch_shapes=[
            pltpu.VMEM((1, grid_n), jnp.int32),
            pltpu.VMEM((1, grid_n), jnp.int32),
            pltpu.SMEM((1, grid_n), jnp.int32),
            pltpu.VMEM((count, 2, blocks), jnp.int32),
            pltpu.VMEM((count, 2, blocks), jnp.int32),
            pltpu.VMEM((1, blocks), jnp.int32),
            pltpu.VMEM((1, blocks), jnp.int32),
            pltpu.VMEM((blocks, width, width), BF),
            *[pltpu.VMEM((blocks, quarter, width), BF)] * near_n,
            pltpu.VMEM((yc_n * 4, near_n, quarter, width), BF),
            pltpu.VMEM((yc_n * 4, near_n, quarter, width), BF),
            pltpu.VMEM((2, steps, yc_n * 4, quarter, width), BF),
            pltpu.VMEM((z_n - near_n, yc_n * 4, quarter, width), BF),
            pltpu.VMEM((2, steps, yc_n * 4, quarter, width), BF),
            pltpu.VMEM((z_n - near_n, yc_n * 4, quarter, width), BF),
            pltpu.VMEM((4, grid_n - (2 * reach - 1 + DIRECT) * yc_n, quarter, width), BF),
            pltpu.VMEM((grid_n, quarter, width), BF),
            pltpu.VMEM((grid_n + 1, width, width), BF),
            pltpu.VMEM((grid_n + 1, width, width), BF),
            pltpu.VMEM((grid_n, quarter, width), BF),
            pltpu.VMEM((blocks, width, width), BF),
            pltpu.VMEM((blocks, width, width), BF),
            pltpu.VMEM((6, blocks, ROWS, width), BF),
            pltpu.VMEM((6, blocks, ROWS, width), BF),
            pltpu.VMEM((2, blocks, ROWS, width), BF),
            pltpu.VMEM((2, blocks, ROWS, width), BF),
            pltpu.VMEM((count, 2, 128), jnp.int32),
            pltpu.SMEM((count, 2, 128), jnp.int32),
            pltpu.VMEM((4, count, 2, 128), jnp.int32),
            pltpu.SMEM((4, count, 2, 128), jnp.int32),
            pltpu.VMEM((near_n, 4, 1, 128), jnp.int32),
            pltpu.SMEM((near_n, 4, 1, 128), jnp.int32),
            dma((5,)),
            dma((5,)),
            dma((2, reach, SUBS)),
            dma((2, reach, SUBS)),
            dma((2, 2, 2 * steps - 1)),
            dma((2, 2, 2 * steps - 1)),
            dma((2, 3)),
            dma((2, 3)),
            dma((3,)),
            dma((3,)),
            dma((2 + z_n,)),
            dma((2 + z_n,)),
            dma((10,)),
            dma((2, 6, CHUNKS)),
            dma((2, 6, CHUNKS)),
        ],
        compiler_params=pltpu.CompilerParams(
            collective_id=0, has_side_effects=True, vmem_limit_bytes=60 * 1024 * 1024
        ),
    )(x_blocks, *small)


def solution(mesh, y_n=4):
    return jax.shard_map(
        functools.partial(local, y_n),
        mesh=mesh,
        in_specs=(
            P("grid", None, None),
            P("grid", "layer", None, None),
            P("grid", "layer", None, None),
            P("grid", None, None),
            P("grid", "layer", None, None),
            P("grid", "layer", None, None),
            P("grid", "layer"),
            P("grid", "layer"),
        ),
        out_specs=(P("grid", "layer", None), P("grid", "layer", None)),
        check_vma=False,
    )
```
